32 devices in a mesh: gx: 4 (over y, core), gy: 2 (over x), gz: 4 (over z).
Axes of the slice: x: 2, y: 2, z: 4, core: 2. Of those that a mesh axis runs over, the one named last changes fastest.
Arguments:
- noise: float32 [32, 16, 16, 512], P(None, 'gx', 'gy', 'gz'), may hold values from -32 to 32
- basis: float32 [192, 16, 16, 512], P(None, 'gx', 'gy', 'gz'), may hold values from -5 to 5
- conductivity: float32 [16, 16, 512], P('gx', 'gy', 'gz'), may hold values from 0.2 to 2
- reaction: float32 [16, 16, 512], P('gx', 'gy', 'gz'), may hold values from 0.05 to 0.5
Outputs:
- new_block: float32 [32, 16, 16, 512], P(None, 'gx', 'gy', 'gz')
- factor: float32 [32, 32], replicated
- projection: float32 [192, 32], replicated
The draws below stay inside these ranges and needn't reach their ends.
All inputs are finite; a program needn't handle non-finite values.
Results may differ from the reference program's by a relative error of at most 0.00012.
Values sent between devices are 32-bit elements; how exact they have to be, the bound alone decides.
A program may use at most 64 MiB of HBM per device.

```python
import math
import jax
import jax.numpy as jnp
from jax import lax

COLS = 32
BLOCKS = 6
BASIS = 192
NX = 16
NY = 16
NZ = 512


def basis_field(seed_key):
    shape = (BASIS, NX, NY, NZ)
    return jnp.clip(jax.random.normal(seed_key, shape), -5.0, 5.0)


def draw_basis(key, part):
    return basis_field(jax.random.fold_in(key, 11))


def draw_noise(key, part):
    stored = basis_field(jax.random.fold_in(key, 11)).reshape(BLOCKS, COLS, NX, NY, NZ)
    weights = jax.random.uniform(jax.random.fold_in(key, 12), (BLOCKS, COLS, 1, 1, 1), minval=0.3, maxval=0.7)
    fresh = jnp.clip(jax.random.normal(jax.random.fold_in(key, 13), (COLS, NX, NY, NZ)), -5.0, 5.0)
    return jnp.sum(weights * stored, axis=0) + 0.8 * fresh


def block_levels(key, shape, pieces, low, top_value):
    factor_of = 1.0
    for axis_at, shards_of in pieces:
        draws = jax.random.uniform(jax.random.fold_in(jax.random.fold_in(key, 6), axis_at), (shards_of,), jnp.float32, low / len(pieces), top_value / len(pieces))
        factor_of = factor_of * jnp.repeat(jnp.exp(draws), shape[axis_at] // shards_of).reshape((-1,) + (1,) * (len(shape) - 1 - axis_at))
    return factor_of


def setup_inputs(seed: int = 0) -> dict:
    splits = jax.random.split(jax.random.key(seed), 5)
    noise = draw_noise(jax.random.fold_in(splits[4], 71), 0)
    basis = draw_basis(jax.random.fold_in(splits[4], 71), 0)
    conductivity = jnp.clip(jnp.exp(math.log(2.0) - 2.3025851 * jax.random.uniform(splits[2], (NX, NY, NZ), jnp.float32) ** block_levels(splits[2], (NX, NY, NZ), ((0, 4), (1, 2), (2, 4)), -0.2, 0.2)), 0.2, 2.0)
    reaction = jnp.clip(jnp.exp(math.log(0.5) - 2.3025851 * jax.random.uniform(splits[3], (NX, NY, NZ), jnp.float32) ** block_levels(splits[3], (NX, NY, NZ), ((0, 4), (1, 2), (2, 4)), -0.2, 0.2)), 0.05, 0.5)
    return dict(noise=noise, basis=basis, conductivity=conductivity, reaction=reaction)


def stencil(field_pad, theta_pad, reaction_core):
    theta_core = theta_pad[1:-1, 1:-1, 1:-1]
    value_core = field_pad[:, 1:-1, 1:-1, 1:-1]
    result = reaction_core * value_core
    diagonal = reaction_core
    offsets = ((slice(2, None), slice(1, -1), slice(1, -1)), (slice(None, -2), slice(1, -1), slice(1, -1)), (slice(1, -1), slice(2, None), slice(1, -1)), (slice(1, -1), slice(None, -2), slice(1, -1)), (slice(1, -1), slice(1, -1), slice(2, None)), (slice(1, -1), slice(1, -1), slice(None, -2)))
    for slicer in offsets:
        face_value = 0.5 * (theta_core + theta_pad[slicer])
        result = result + face_value * (value_core - field_pad[(slice(None),) + slicer])
        diagonal = diagonal + face_value
    return (result, diagonal)

def reference(noise, basis, conductivity, reaction):
    highest = lax.Precision.HIGHEST
    cell_total = float(NX * NY * NZ)
    theta_pad = jnp.pad(conductivity, 1)
    widths = ((0, 0), (1, 1), (1, 1), (1, 1))
    first, diagonal = stencil(jnp.pad(noise, widths), theta_pad, reaction)
    scaled = first / diagonal
    image, unused = stencil(jnp.pad(scaled, widths), theta_pad, reaction)
    basis_flat = basis.reshape(BASIS, -1)
    image_flat = image.reshape(COLS, -1)

    def inner_product(left, right):
        return lax.dot_general(left, right, (((1,), (1,)), ((), ())), precision=highest) / cell_total

    def remove(block, coeff):
        return block - lax.dot_general(coeff, basis_flat, (((0,), (0,)), ((), ())), precision=highest)
    coeff_one = inner_product(basis_flat, image_flat)
    image_one = remove(image_flat, coeff_one)
    coeff_two = inner_product(basis_flat, image_one)
    image_two = remove(image_one, coeff_two)
    lower_one = jnp.linalg.cholesky(inner_product(image_two, image_two))
    middle = jax.scipy.linalg.solve_triangular(lower_one, image_two, lower=True)
    lower_two = jnp.linalg.cholesky(inner_product(middle, middle))
    new_block = jax.scipy.linalg.solve_triangular(lower_two, middle, lower=True)
    factor = jnp.dot(lower_two.T, lower_one.T, precision=highest)
    return (new_block.reshape(noise.shape), factor, coeff_one + coeff_two)
```

```python
import functools

import jax
import jax.numpy as jnp
from jax import lax
from jax.experimental import pallas as pl
from jax.experimental.pallas import tpu as pltpu
from jax.sharding import PartitionSpec as P

MESH = pl.DeviceIdType.MESH
GROUP = 8
F32 = jnp.float32
BF16 = jnp.bfloat16


def each(count, body):
    if count <= 8:
        for k in range(1, count):
            body(k)
    else:
        lax.fori_loop(1, count, lambda k, c: (body(k), c)[1], 0)


class Team:
    def __init__(self, axes, sizes):
        self.axes = axes
        self.sizes = sizes
        self.count = 1
        for axis in axes:
            self.count *= sizes[axis]

    def me(self):
        index = 0
        for axis in self.axes:
            index = index * self.sizes[axis] + lax.axis_index(axis)
        return index

    def device(self, index):
        out = {}
        for axis in reversed(self.axes):
            out[axis] = lax.rem(index, self.sizes[axis])
            index = lax.div(index, self.sizes[axis])
        return out

    def peer(self, k):
        return lax.rem(self.me() + k, self.count)


class Sum:
    def __init__(self, owners, others, data, landed, crossed, result, sems):
        self.owners, self.others = owners, others
        self.data, self.landed, self.crossed, self.result = data, landed, crossed, result
        self.sems = sems
        self.share = data.shape[0] // owners.count

    def copy(self, phase, team, src, dst_ref, slot, peer):
        send, recv = self.sems[2 * phase], self.sems[2 * phase + 1]
        return pltpu.make_async_remote_copy(
            src_ref=src,
            dst_ref=dst_ref.at[slot],
            send_sem=send.at[peer],
            recv_sem=recv.at[slot],
            device_id=team.device(peer),
            device_id_type=MESH,
        )

    def piece(self, index):
        return self.data.at[pl.ds(index * self.share, self.share)]

    def scatter(self):
        team, me = self.owners, self.owners.me()

        def go(k):
            peer = team.peer(k)
            self.copy(0, team, self.piece(peer), self.landed, me, peer).start()

        each(team.count, go)
        self.landed[me] = self.data[pl.ds(me * self.share, self.share)]

    def settle(self, phase, team, src, dst_ref):
        def go(k):
            peer = team.peer(k)
            self.copy(phase, team, src, dst_ref, peer, peer).wait_recv()

        each(team.count, go)

    def cross(self):
        self.settle(0, self.owners, self.piece(0), self.landed)
        team, me = self.others, self.others.me()
        total = self.landed[0]
        for k in range(1, self.owners.count):
            total = total + self.landed[k]
        self.crossed[me] = total

        def go(k):
            peer = team.peer(k)
            self.copy(1, team, self.crossed.at[me], self.crossed, me, peer).start()

        each(team.count, go)

    def gather(self):
        self.settle(1, self.others, self.crossed.at[0], self.crossed)
        team, me = self.owners, self.owners.me()
        total = self.crossed[0]
        for k in range(1, self.others.count):
            total = total + self.crossed[k]
        self.result[me] = total

        def go(k):
            peer = team.peer(k)
            self.copy(2, team, self.result.at[me], self.result, me, peer).start()

        each(team.count, go)

    def finish(self):
        self.settle(2, self.owners, self.result.at[0], self.result)

    def drain(self):
        def scattered(k):
            peer = self.owners.peer(k)
            self.copy(0, self.owners, self.piece(0), self.landed, 0, peer).wait_send()

        def crossed(k):
            peer = self.others.peer(k)
            self.copy(1, self.others, self.crossed.at[0], self.crossed, 0, peer).wait_send()

        def gathered(k):
            peer = self.owners.peer(k)
            self.copy(2, self.owners, self.result.at[0], self.result, 0, peer).wait_send()

        each(self.owners.count, scattered)
        each(self.others.count, crossed)
        each(self.owners.count, gathered)


class Rim:
    def __init__(self, field, x_in, y_out, y_in, z_out, z_in, send, recv, sizes):
        self.sizes = sizes
        self.send, self.recv = send, recv
        last = field.shape[1] - 1
        self.routes = (
            ("gx", (field.at[:, 0], field.at[:, last]), x_in),
            ("gy", (y_out.at[0], y_out.at[1]), y_in),
            ("gz", (z_out.at[0], z_out.at[1]), z_in),
        )

    def exists(self, axis, side):
        me = lax.axis_index(axis)
        return me > 0 if side == 0 else me < self.sizes[axis] - 1

    def copy(self, at, side):
        axis, out, into = self.routes[at]
        me = lax.axis_index(axis)
        step = -1 if side == 0 else 1
        return pltpu.make_async_remote_copy(
            src_ref=out[side],
            dst_ref=into.at[1 - side],
            send_sem=self.send.at[2 * at + side],
            recv_sem=self.recv.at[2 * at + 1 - side],
            device_id={axis: me + step},
            device_id_type=MESH,
        )

    def start(self, at):
        axis = self.routes[at][0]
        for side in range(2):
            pl.when(self.exists(axis, side))(lambda at=at, side=side: self.copy(at, side).start())

    def blank(self):
        for axis, _, into in self.routes:
            for side in range(2):
                @pl.when(jnp.logical_not(self.exists(axis, side)))
                def _(into=into, side=side):
                    into[side] = jnp.zeros(into.shape[1:], F32)

    def arrive(self):
        for at in range(3):
            axis = self.routes[at][0]
            for side in range(2):
                pl.when(self.exists(axis, side))(
                    lambda at=at, side=side: self.copy(at, 1 - side).wait_recv()
                )

    def drain(self):
        for at in range(3):
            axis = self.routes[at][0]
            for side in range(2):
                pl.when(self.exists(axis, side))(
                    lambda at=at, side=side: self.copy(at, side).wait_send()
                )


def lanes_of(shape):
    return lax.broadcasted_iota(jnp.int32, shape, len(shape) - 1)


def pack_y(flat, rows, y_out):
    for side, first in ((0, 0), (1, 7)):
        y_out[side, pl.ds(0, rows), :] = flat[pl.ds(first, rows, stride=8), :]


def pack_z(tiles, lanes_total):
    lane = lanes_of((8, 128))
    lo = jnp.zeros((8, 128), F32)
    hi = jnp.zeros((8, 128), F32)
    for i in range(lanes_total):
        tile = tiles[i]
        lo = jnp.where(lane == i, jnp.broadcast_to(tile[:, 0:1], (8, 128)), lo)
        hi = jnp.where(lane == i, jnp.broadcast_to(tile[:, 127:128], (8, 128)), hi)
    return lo, hi


def neighbours(value, x_lo, x_hi, y_lo, y_hi, z_lo, z_hi):
    count, span = value.shape[0], value.shape[1]
    tiles = count * span
    flat = value.reshape(tiles, 8, 128)
    below = jnp.concatenate([x_lo[:, None], value[:, : span - 1]], axis=1)
    above = jnp.concatenate([value[:, 1:], x_hi[:, None]], axis=1)
    row = lax.broadcasted_iota(jnp.int32, (8, 128), 0)
    lane = lanes_of((8, 128))
    before, after, left, right = [], [], [], []
    for i in range(tiles):
        tile = flat[i]
        before.append(
            jnp.where(row == 0, jnp.broadcast_to(y_lo[i], (8, 128)), pltpu.roll(tile, 1, 0))
        )
        after.append(
            jnp.where(row == 7, jnp.broadcast_to(y_hi[i], (8, 128)), pltpu.roll(tile, 7, 0))
        )
        left.append(
            jnp.where(lane == 0, jnp.broadcast_to(z_lo[:, i : i + 1], (8, 128)), pltpu.roll(tile, 1, 1))
        )
        right.append(
            jnp.where(
                lane == 127, jnp.broadcast_to(z_hi[:, i : i + 1], (8, 128)), pltpu.roll(tile, 127, 1)
            )
        )
    join = lambda parts: jnp.stack(parts).reshape(value.shape)
    return above, below, join(after), join(before), join(right), join(left)


def split(value):
    high = value.astype(BF16)
    return high, (value - high.astype(F32)).astype(BF16)


def dot(left, right, dims):
    return lax.dot_general(left, right, (dims, ((), ())), preferred_element_type=F32)


def dot_full(left, right, dims):
    return lax.dot_general(
        left, right, (dims, ((), ())), precision=lax.Precision.HIGHEST, preferred_element_type=F32
    )


NT = ((1,), (1,))
NN = ((1,), (0,))


def kernel(sizes, owners, others, cell_total, noise, basis, cond, react, out, factor, proj, *scratch):
    (field, field2, image, stored, react_v, coef, high, low, flat_image, residual, chol,
     x_in1, x_in2, y_out1, y_in1, y_out2, y_in2, z_out1, z_in1, z_out2, z_in2,
     c_data, c_landed, c_crossed, c_result, g_data, g_landed, g_crossed, g_result,
     in_sems, h_send1, h_recv1, h_send2, h_recv2, *sum_sems) = scratch
    columns, span = field2.shape[0], field2.shape[1]
    plane = span * 8
    kept = basis.shape[0] // plane
    cells = plane * 128
    tiles = columns * span
    scale = 1.0 / cell_total

    load_noise = pltpu.make_async_copy(noise, field.at[pl.ds(0, columns)], in_sems.at[0])
    load_cond = pltpu.make_async_copy(cond, field.at[columns], in_sems.at[1])
    load_react = pltpu.make_async_copy(react, react_v, in_sems.at[2])
    load_basis = pltpu.make_async_copy(basis, stored, in_sems.at[3])
    load_noise.start()
    load_cond.start()
    load_react.start()
    load_basis.start()

    barrier = pltpu.get_barrier_semaphore()
    for team in (owners, others):
        def greet(k, team=team):
            pl.semaphore_signal(
                barrier, inc=1, device_id=team.device(team.peer(k)), device_id_type=MESH
            )
        each(team.count, greet)

    rim1 = Rim(field, x_in1, y_out1, y_in1, z_out1, z_in1, h_send1, h_recv1, sizes)
    rim2 = Rim(field2, x_in2, y_out2, y_in2, z_out2, z_in2, h_send2, h_recv2, sizes)
    rim1.blank()
    rim2.blank()
    load_noise.wait()
    load_cond.wait()
    pl.semaphore_wait(barrier, owners.count + others.count - 2)
    rim1.start(0)
    field_flat = field.reshape((columns + 1) * plane, 128)
    y_rows = tiles + span
    y_out1[...] = jnp.zeros(y_out1.shape, F32)
    pack_y(field_flat, y_rows, y_out1)
    rim1.start(1)
    lo, hi = pack_z(field[0:columns].reshape(tiles, 8, 128), tiles)
    z_out1[0, 0], z_out1[1, 0] = lo, hi
    lo, hi = pack_z(field[columns], span)
    z_out1[0, 1], z_out1[1, 1] = lo, hi
    rim1.start(2)

    load_basis.wait()
    spare = high.shape[0] - kept
    high[kept:, :] = jnp.zeros((spare, cells), BF16)
    low[kept:, :] = jnp.zeros((spare, cells), BF16)
    for at in range(plane):
        one, two = split(stored[pl.ds(at, kept, stride=plane), :])
        high[0:kept, at * 128 : (at + 1) * 128] = one
        low[0:kept, at * 128 : (at + 1) * 128] = two

    chunk = 1024
    g_one = jnp.zeros((kept, 256), F32)
    g_two = jnp.zeros((kept, 256), F32)
    for at in range(0, cells, chunk):
        right = high[:, at : at + chunk]
        g_one = g_one + dot(high[0:kept, at : at + chunk], right, NT)
        g_two = g_two + dot(low[0:kept, at : at + chunk], right, NT)
    turned = jnp.transpose(jnp.concatenate([g_two, jnp.zeros((256 - kept, 256), F32)], axis=0))
    g_local = g_one + g_two + turned[0:kept]
    for at in range(kept // 8):
        for half in range(2):
            g_data[2 * at + half] = g_local[8 * at : 8 * at + 8, 128 * half : 128 * half + 128]

    c_sum = Sum(owners, others, c_data, c_landed, c_crossed, c_result, sum_sems[0:6])
    g_sum = Sum(owners, others, g_data, g_landed, g_crossed, g_result, sum_sems[6:12])
    g_sum.scatter()

    load_react.wait()
    rim1.arrive()
    theta = field[columns]
    around = neighbours(
        theta[None],
        x_in1[0, columns][None],
        x_in1[1, columns][None],
        [y_in1[0, pl.ds(tiles + i, 1), :] for i in range(span)],
        [y_in1[1, pl.ds(tiles + i, 1), :] for i in range(span)],
        z_in1[0, 1],
        z_in1[1, 1],
    )
    diagonal = react_v[...]
    for face, other in enumerate(around):
        value = 0.5 * (theta + other[0])
        coef[face] = value
        diagonal = diagonal + value
    coef[6] = diagonal

    def apply(source, x_in, y_in, z_in, group):
        start = group * GROUP
        value = source[pl.ds(start, GROUP)]
        shift = lax.rem(128 - group * (GROUP * span), 128)
        first = start * span
        around = neighbours(
            value,
            x_in[0, pl.ds(start, GROUP)],
            x_in[1, pl.ds(start, GROUP)],
            [y_in[0, pl.ds(first + i, 1), :] for i in range(GROUP * span)],
            [y_in[1, pl.ds(first + i, 1), :] for i in range(GROUP * span)],
            pltpu.roll(z_in[0, 0], shift, 1),
            pltpu.roll(z_in[1, 0], shift, 1),
        )
        result = react_v[...][None] * value
        for face, other in enumerate(around):
            result = result + coef[face][None] * (value - other)
        return start, result

    def first_step(group, carry):
        start, result = apply(field, x_in1, y_in1, z_in1, group)
        field2[pl.ds(start, GROUP)] = result / coef[6][None]
        return carry

    lax.fori_loop(0, columns // GROUP, first_step, 0)
    rim2.start(0)
    pack_y(field2.reshape(columns * plane, 128), tiles, y_out2)
    rim2.start(1)
    lo, hi = pack_z(field2[...].reshape(tiles, 8, 128), tiles)
    z_out2[0, 0], z_out2[1, 0] = lo, hi
    rim2.start(2)
    g_sum.cross()
    rim2.arrive()

    def second_step(group, carry):
        start, result = apply(field2, x_in2, y_in2, z_in2, group)
        image[pl.ds(start, GROUP)] = result
        return carry

    lax.fori_loop(0, columns // GROUP, second_step, 0)
    image_rows = image.reshape(columns * plane, 128)
    for at in range(plane):
        value = image_rows[pl.ds(at, columns, stride=plane), :]
        flat_image[:, at * 128 : (at + 1) * 128] = value
        one, two = split(value)
        high[kept : kept + columns, at * 128 : (at + 1) * 128] = one
        low[kept : kept + columns, at * 128 : (at + 1) * 128] = two

    both = jnp.zeros((2 * columns, 256), F32)
    for at in range(0, cells, chunk):
        here = slice(at, at + chunk)
        left = jnp.concatenate([high[kept : kept + columns, here], low[kept : kept + columns, here]], axis=0)
        both = both + dot(left, high[:, here], NT) + dot(left, low[:, here], NT)
    c_local = both[0:columns] + both[columns:]
    for at in range(columns // 8):
        for half in range(2):
            c_data[2 * at + half] = c_local[8 * at : 8 * at + 8, 128 * half : 128 * half + 128]
    c_sum.scatter()
    g_sum.gather()
    c_sum.cross()
    c_sum.gather()
    g_sum.finish()
    c_sum.finish()

    def whole(total, rows):
        tiles_of = total[...].reshape(rows // 4, 8, 128)
        return jnp.concatenate(
            [
                jnp.concatenate([tiles_of[2 * at], tiles_of[2 * at + 1]], axis=1)
                for at in range(rows // 8)
            ],
            axis=0,
        )

    g_full = jnp.concatenate(
        [whole(g_result, kept) * scale, jnp.zeros((256 - kept, 256), F32)], axis=0
    )
    c_full = whole(c_result, columns) * scale
    lane = lanes_of((columns, 256))
    c_one = jnp.where(lane < kept, c_full, 0.0)
    square = c_full[:, kept : kept + columns]
    total = 2.0 * c_one - dot_full(c_one, g_full, NN)
    rest = c_one - dot_full(total, g_full, NN)
    gram = square - dot_full(c_one, total, NT) - dot_full(total, rest, NT)
    proj[...] = jnp.transpose(total)[0:kept, :]

    p_high, p_low = split(total)
    p_both = jnp.concatenate([p_high, p_low], axis=0)[:, 0:kept]
    for at in range(0, cells, chunk):
        here = slice(at, at + chunk)
        part = dot(p_both, high[0:kept, here], NN) + dot(p_both, low[0:kept, here], NN)
        residual[:, here] = flat_image[:, here] - part[0:columns] - part[columns:]

    wide = (columns, 128)
    lane = lanes_of(wide)
    row = lax.broadcasted_iota(jnp.int32, wide, 0)
    table = jnp.where(lane == row + columns, 1.0, 0.0).astype(F32)
    table = table + jnp.concatenate([gram, jnp.zeros((columns, 128 - columns), F32)], axis=1)
    for k in range(columns):
        column = jnp.broadcast_to(table[:, k : k + 1], wide)
        root = lax.rsqrt(column[k : k + 1, :])
        line = table[k : k + 1, :] * root
        chol[k : k + 1, :] = line
        table = table - (column * root) * line
    done = chol[...]
    factor[...] = jnp.where(lane >= row, done, 0.0)[:, 0:columns]
    inverse = done[:, columns : 2 * columns]
    for at in range(0, cells, chunk):
        here = slice(at, at + chunk)
        part = dot_full(inverse, residual[:, here], NN)
        for k in range(chunk // 128):
            out[pl.ds(at // 128 + k, columns, stride=plane), :] = part[:, 128 * k : 128 * k + 128]

    rim1.drain()
    rim2.drain()
    g_sum.drain()
    c_sum.drain()


def shards(sizes, noise, basis, cond, react):
    columns, span, rows, lanes = noise.shape
    kept = basis.shape[0]
    plane = span * rows
    cells = plane * lanes
    cell_total = float(cells * sizes["gx"] * sizes["gy"] * sizes["gz"])
    c_tiles, g_tiles = columns // 4, kept // 4
    own, rest, count = [], [], 1
    for axis in ("gx", "gy", "gz"):
        if c_tiles % (count * sizes[axis]) == 0:
            count *= sizes[axis]
            own.append(axis)
        else:
            rest.append(axis)
    owners, others = Team(own, sizes), Team(rest, sizes)
    vmem = lambda *shape: pltpu.VMEM(shape, F32)
    y_rows = -(-(columns + 1) * span // 8) * 8

    def sum_buffers(tiles):
        share = tiles // owners.count
        return [
            vmem(tiles, 8, 128),
            vmem(owners.count, share, 8, 128),
            vmem(others.count, share, 8, 128),
            vmem(owners.count, share, 8, 128),
        ]

    dma = lambda n: pltpu.SemaphoreType.DMA((n,))
    sum_sems = [dma(n) for n in (owners.count, owners.count, others.count, others.count, owners.count, owners.count)]
    scratch = [
        vmem(columns + 1, span, 8, 128),
        vmem(columns, span, 8, 128),
        vmem(columns, span, 8, 128),
        vmem(kept * plane, 128),
        vmem(span, 8, 128),
        vmem(7, span, 8, 128),
        pltpu.VMEM((256, cells), BF16),
        pltpu.VMEM((256, cells), BF16),
        vmem(columns, cells),
        vmem(columns, cells),
        vmem(columns, 128),
        vmem(2, columns + 1, 8, 128),
        vmem(2, columns, 8, 128),
        vmem(2, y_rows, 128),
        vmem(2, y_rows, 128),
        vmem(2, columns * span, 128),
        vmem(2, columns * span, 128),
        vmem(2, 2, 8, 128),
        vmem(2, 2, 8, 128),
        vmem(2, 1, 8, 128),
        vmem(2, 1, 8, 128),
        *sum_buffers(c_tiles),
        *sum_buffers(g_tiles),
        dma(4),
        dma(6),
        dma(6),
        dma(6),
        dma(6),
        *sum_sems,
        *sum_sems,
    ]
    out, factor, proj = pl.pallas_call(
        functools.partial(kernel, sizes, owners, others, cell_total),
        out_shape=(
            jax.ShapeDtypeStruct((columns * plane, lanes), F32),
            jax.ShapeDtypeStruct((columns, columns), F32),
            jax.ShapeDtypeStruct((kept, columns), F32),
        ),
        in_specs=[pl.BlockSpec(memory_space=pl.ANY)] * 4,
        out_specs=tuple([pl.BlockSpec(memory_space=pltpu.VMEM)] * 3),
        scratch_shapes=scratch,
        compiler_params=pltpu.CompilerParams(
            collective_id=0, has_side_effects=True, vmem_limit_bytes=48 * 1024 * 1024
        ),
        name="lanczos_step",
    )(noise, basis.reshape(kept * plane, lanes), cond, react)
    return out.reshape(noise.shape), factor, proj


def solution(mesh):
    sizes = dict(mesh.shape)
    return jax.shard_map(
        functools.partial(shards, sizes),
        mesh=mesh,
        in_specs=(
            P(None, "gx", "gy", "gz"),
            P(None, "gx", "gy", "gz"),
            P("gx", "gy", "gz"),
            P("gx", "gy", "gz"),
        ),
        out_specs=(P(None, "gx", "gy", "gz"), P(), P()),
        check_vma=False,
    )
```

```python
import functools

import jax
import jax.numpy as jnp
from jax import lax
from jax.experimental import pallas as pl
from jax.experimental.pallas import tpu as pltpu
from jax.sharding import PartitionSpec as P

MESH = pl.DeviceIdType.MESH
GROUP = 8
VMEM_GRANT = 63 * 1024 * 1024
F32 = jnp.float32
BF16 = jnp.bfloat16


def each(count, body):
    if count <= 8:
        for k in range(1, count):
            body(k)
    else:
        lax.fori_loop(1, count, lambda k, c: (body(k), c)[1], 0)


class Team:
    def __init__(self, axes, sizes):
        self.axes = axes
        self.sizes = sizes
        self.count = 1
        for axis in axes:
            self.count *= sizes[axis]

    def me(self):
        index = 0
        for axis in self.axes:
            index = index * self.sizes[axis] + lax.axis_index(axis)
        return index

    def device(self, index):
        out = {}
        for axis in reversed(self.axes):
            out[axis] = lax.rem(index, self.sizes[axis])
            index = lax.div(index, self.sizes[axis])
        return out

    def peer(self, k):
        return lax.rem(self.me() + k, self.count)


class Sum:
    def __init__(self, owners, others, data, landed, crossed, result, sems):
        self.owners, self.others = owners, others
        self.data, self.landed, self.crossed, self.result = data, landed, crossed, result
        self.sems = sems
        self.share = data.shape[0] // owners.count

    def copy(self, phase, team, src, dst_ref, slot, peer):
        send, recv = self.sems[2 * phase], self.sems[2 * phase + 1]
        return pltpu.make_async_remote_copy(
            src_ref=src,
            dst_ref=dst_ref.at[slot],
            send_sem=send.at[peer],
            recv_sem=recv.at[slot],
            device_id=team.device(peer),
            device_id_type=MESH,
        )

    def piece(self, index):
        return self.data.at[pl.ds(index * self.share, self.share)]

    def scatter(self):
        team, me = self.owners, self.owners.me()

        def go(k):
            peer = team.peer(k)
            self.copy(0, team, self.piece(peer), self.landed, me, peer).start()

        each(team.count, go)
        self.landed[me] = self.data[pl.ds(me * self.share, self.share)]

    def settle(self, phase, team, src, dst_ref):
        def go(k):
            peer = team.peer(k)
            self.copy(phase, team, src, dst_ref, peer, peer).wait_recv()

        each(team.count, go)

    def cross(self):
        self.settle(0, self.owners, self.piece(0), self.landed)
        team, me = self.others, self.others.me()
        total = self.landed[0]
        for k in range(1, self.owners.count):
            total = total + self.landed[k]
        self.crossed[me] = total

        def go(k):
            peer = team.peer(k)
            self.copy(1, team, self.crossed.at[me], self.crossed, me, peer).start()

        each(team.count, go)

    def gather(self):
        self.settle(1, self.others, self.crossed.at[0], self.crossed)
        team, me = self.owners, self.owners.me()
        total = self.crossed[0]
        for k in range(1, self.others.count):
            total = total + self.crossed[k]
        self.result[me] = total

        def go(k):
            peer = team.peer(k)
            self.copy(2, team, self.result.at[me], self.result, me, peer).start()

        each(team.count, go)

    def finish(self):
        self.settle(2, self.owners, self.result.at[0], self.result)

    def drain(self):
        def scattered(k):
            peer = self.owners.peer(k)
            self.copy(0, self.owners, self.piece(0), self.landed, 0, peer).wait_send()

        def crossed(k):
            peer = self.others.peer(k)
            self.copy(1, self.others, self.crossed.at[0], self.crossed, 0, peer).wait_send()

        def gathered(k):
            peer = self.owners.peer(k)
            self.copy(2, self.owners, self.result.at[0], self.result, 0, peer).wait_send()

        each(self.owners.count, scattered)
        each(self.others.count, crossed)
        each(self.owners.count, gathered)


class Rim:
    def __init__(self, field, x_in, y_out, y_in, z_out, z_in, send, recv, sizes):
        self.sizes = sizes
        self.send, self.recv = send, recv
        last = field.shape[1] - 1
        self.routes = (
            ("gx", (field.at[:, 0], field.at[:, last]), x_in),
            ("gy", (y_out.at[0], y_out.at[1]), y_in),
            ("gz", (z_out.at[0], z_out.at[1]), z_in),
        )

    def exists(self, axis, side):
        me = lax.axis_index(axis)
        return me > 0 if side == 0 else me < self.sizes[axis] - 1

    def copy(self, at, side):
        axis, out, into = self.routes[at]
        me = lax.axis_index(axis)
        step = -1 if side == 0 else 1
        return pltpu.make_async_remote_copy(
            src_ref=out[side],
            dst_ref=into.at[1 - side],
            send_sem=self.send.at[2 * at + side],
            recv_sem=self.recv.at[2 * at + 1 - side],
            device_id={axis: me + step},
            device_id_type=MESH,
        )

    def start(self, at):
        axis = self.routes[at][0]
        for side in range(2):
            pl.when(self.exists(axis, side))(lambda at=at, side=side: self.copy(at, side).start())

    def blank(self):
        for axis, _, into in self.routes:
            for side in range(2):
                @pl.when(jnp.logical_not(self.exists(axis, side)))
                def _(into=into, side=side):
                    into[side] = jnp.zeros(into.shape[1:], F32)

    def arrive(self):
        for at in range(3):
            axis = self.routes[at][0]
            for side in range(2):
                pl.when(self.exists(axis, side))(
                    lambda at=at, side=side: self.copy(at, 1 - side).wait_recv()
                )

    def drain(self):
        for at in range(3):
            axis = self.routes[at][0]
            for side in range(2):
                pl.when(self.exists(axis, side))(
                    lambda at=at, side=side: self.copy(at, side).wait_send()
                )


def lanes_of(shape):
    return lax.broadcasted_iota(jnp.int32, shape, len(shape) - 1)


def pack_y(flat, rows, y_out):
    for side, first in ((0, 0), (1, 7)):
        y_out[side, pl.ds(0, rows), :] = flat[pl.ds(first, rows, stride=8), :]


def pack_z(tiles, lanes_total):
    lane = lanes_of((8, 128))
    lo = jnp.zeros((8, 128), F32)
    hi = jnp.zeros((8, 128), F32)
    for i in range(lanes_total):
        tile = tiles[i]
        lo = jnp.where(lane == i, jnp.broadcast_to(tile[:, 0:1], (8, 128)), lo)
        hi = jnp.where(lane == i, jnp.broadcast_to(tile[:, 127:128], (8, 128)), hi)
    return lo, hi


def neighbours(value, x_lo, x_hi, y_lo, y_hi, z_lo, z_hi):
    count, span = value.shape[0], value.shape[1]
    tiles = count * span
    flat = value.reshape(tiles, 8, 128)
    below = jnp.concatenate([x_lo[:, None], value[:, : span - 1]], axis=1)
    above = jnp.concatenate([value[:, 1:], x_hi[:, None]], axis=1)
    row = lax.broadcasted_iota(jnp.int32, (8, 128), 0)
    lane = lanes_of((8, 128))
    before, after, left, right = [], [], [], []
    for i in range(tiles):
        tile = flat[i]
        before.append(
            jnp.where(row == 0, jnp.broadcast_to(y_lo[i], (8, 128)), pltpu.roll(tile, 1, 0))
        )
        after.append(
            jnp.where(row == 7, jnp.broadcast_to(y_hi[i], (8, 128)), pltpu.roll(tile, 7, 0))
        )
        left.append(
            jnp.where(lane == 0, jnp.broadcast_to(z_lo[:, i : i + 1], (8, 128)), pltpu.roll(tile, 1, 1))
        )
        right.append(
            jnp.where(
                lane == 127, jnp.broadcast_to(z_hi[:, i : i + 1], (8, 128)), pltpu.roll(tile, 127, 1)
            )
        )
    join = lambda parts: jnp.stack(parts).reshape(value.shape)
    return above, below, join(after), join(before), join(right), join(left)


def split(value):
    high = value.astype(BF16)
    return high, (value - high.astype(F32)).astype(BF16)


def dot(left, right, dims):
    return lax.dot_general(left, right, (dims, ((), ())), preferred_element_type=F32)


def dot_full(left, right, dims):
    return lax.dot_general(
        left, right, (dims, ((), ())), precision=lax.Precision.HIGHEST, preferred_element_type=F32
    )


NT = ((1,), (1,))
NN = ((1,), (0,))


def kernel(sizes, owners, others, cell_total, noise, basis, cond, react, out, factor, proj, *scratch):
    (field, field2, image, stored, react_v, coef, high, low, flat_image, residual, chol,
     x_in1, x_in2, y_out1, y_in1, y_out2, y_in2, z_out1, z_in1, z_out2, z_in2,
     c_data, c_landed, c_crossed, c_result, g_data, g_landed, g_crossed, g_result,
     in_sems, out_sems, h_send1, h_recv1, h_send2, h_recv2, *sum_sems) = scratch
    columns, span = field2.shape[0], field2.shape[1]
    plane = span * 8
    kept = basis.shape[0] // plane
    cells = plane * 128
    tiles = columns * span
    scale = 1.0 / cell_total

    load_noise = pltpu.make_async_copy(noise, field.at[pl.ds(0, columns)], in_sems.at[0])
    load_cond = pltpu.make_async_copy(cond, field.at[columns], in_sems.at[1])
    load_react = pltpu.make_async_copy(react, react_v, in_sems.at[2])
    load_basis = pltpu.make_async_copy(basis, stored, in_sems.at[3])
    load_noise.start()
    load_cond.start()
    load_react.start()
    load_basis.start()

    barrier = pltpu.get_barrier_semaphore()
    for team in (owners, others):
        def greet(k, team=team):
            pl.semaphore_signal(
                barrier, inc=1, device_id=team.device(team.peer(k)), device_id_type=MESH
            )
        each(team.count, greet)

    rim1 = Rim(field, x_in1, y_out1, y_in1, z_out1, z_in1, h_send1, h_recv1, sizes)
    rim2 = Rim(field2, x_in2, y_out2, y_in2, z_out2, z_in2, h_send2, h_recv2, sizes)
    rim1.blank()
    rim2.blank()
    load_noise.wait()
    load_cond.wait()
    pl.semaphore_wait(barrier, owners.count + others.count - 2)
    rim1.start(0)
    field_flat = field.reshape((columns + 1) * plane, 128)
    y_rows = tiles + span
    y_out1[...] = jnp.zeros(y_out1.shape, F32)
    pack_y(field_flat, y_rows, y_out1)
    rim1.start(1)
    lo, hi = pack_z(field[0:columns].reshape(tiles, 8, 128), tiles)
    z_out1[0, 0], z_out1[1, 0] = lo, hi
    lo, hi = pack_z(field[columns], span)
    z_out1[0, 1], z_out1[1, 1] = lo, hi
    rim1.start(2)

    load_basis.wait()
    spare = high.shape[0] - kept
    high[kept:, :] = jnp.zeros((spare, cells), BF16)
    low[kept:, :] = jnp.zeros((spare, cells), BF16)
    for at in range(plane):
        one, two = split(stored[pl.ds(at, kept, stride=plane), :])
        high[0:kept, at * 128 : (at + 1) * 128] = one
        low[0:kept, at * 128 : (at + 1) * 128] = two

    load_react.wait()
    rim1.arrive()
    theta = field[columns]
    around = neighbours(
        theta[None],
        x_in1[0, columns][None],
        x_in1[1, columns][None],
        [y_in1[0, pl.ds(tiles + i, 1), :] for i in range(span)],
        [y_in1[1, pl.ds(tiles + i, 1), :] for i in range(span)],
        z_in1[0, 1],
        z_in1[1, 1],
    )
    diagonal = react_v[...]
    for face, other in enumerate(around):
        value = 0.5 * (theta + other[0])
        coef[face] = value
        diagonal = diagonal + value
    coef[6] = diagonal

    def apply(source, x_in, y_in, z_in, group):
        start = group * GROUP
        value = source[pl.ds(start, GROUP)]
        shift = lax.rem(128 - group * (GROUP * span), 128)
        first = start * span
        around = neighbours(
            value,
            x_in[0, pl.ds(start, GROUP)],
            x_in[1, pl.ds(start, GROUP)],
            [y_in[0, pl.ds(first + i, 1), :] for i in range(GROUP * span)],
            [y_in[1, pl.ds(first + i, 1), :] for i in range(GROUP * span)],
            pltpu.roll(z_in[0, 0], shift, 1),
            pltpu.roll(z_in[1, 0], shift, 1),
        )
        result = react_v[...][None] * value
        for face, other in enumerate(around):
            result = result + coef[face][None] * (value - other)
        return start, result

    def first_step(group, carry):
        start, result = apply(field, x_in1, y_in1, z_in1, group)
        field2[pl.ds(start, GROUP)] = result / coef[6][None]
        return carry

    lax.fori_loop(0, columns // GROUP, first_step, 0)
    rim2.start(0)
    pack_y(field2.reshape(columns * plane, 128), tiles, y_out2)
    rim2.start(1)
    lo, hi = pack_z(field2[...].reshape(tiles, 8, 128), tiles)
    z_out2[0, 0], z_out2[1, 0] = lo, hi
    rim2.start(2)

    chunk = 1024
    g_one = jnp.zeros((kept, 256), F32)
    g_two = jnp.zeros((kept, 256), F32)
    for at in range(0, cells, chunk):
        right = high[:, at : at + chunk]
        g_one = g_one + dot(high[0:kept, at : at + chunk], right, NT)
        g_two = g_two + dot(low[0:kept, at : at + chunk], right, NT)
    turned = jnp.transpose(jnp.concatenate([g_two, jnp.zeros((256 - kept, 256), F32)], axis=0))
    g_local = g_one + g_two + turned[0:kept]
    for at in range(kept // 8):
        for half in range(2):
            g_data[2 * at + half] = g_local[8 * at : 8 * at + 8, 128 * half : 128 * half + 128]

    c_sum = Sum(owners, others, c_data, c_landed, c_crossed, c_result, sum_sems[0:6])
    g_sum = Sum(owners, others, g_data, g_landed, g_crossed, g_result, sum_sems[6:12])
    g_sum.scatter()

    rim2.arrive()

    def second_step(group, carry):
        start, result = apply(field2, x_in2, y_in2, z_in2, group)
        image[pl.ds(start, GROUP)] = result
        return carry

    lax.fori_loop(0, columns // GROUP, second_step, 0)
    image_rows = image.reshape(columns * plane, 128)
    for at in range(plane):
        value = image_rows[pl.ds(at, columns, stride=plane), :]
        flat_image[:, at * 128 : (at + 1) * 128] = value
        one, two = split(value)
        high[kept : kept + columns, at * 128 : (at + 1) * 128] = one
        low[kept : kept + columns, at * 128 : (at + 1) * 128] = two

    both = jnp.zeros((2 * columns, 256), F32)
    for at in range(0, cells, chunk):
        here = slice(at, at + chunk)
        left = jnp.concatenate([high[kept : kept + columns, here], low[kept : kept + columns, here]], axis=0)
        both = both + dot(left, high[:, here], NT) + dot(left, low[:, here], NT)
    c_local = both[0:columns] + both[columns:]
    for at in range(columns // 8):
        for half in range(2):
            c_data[2 * at + half] = c_local[8 * at : 8 * at + 8, 128 * half : 128 * half + 128]
    g_sum.cross()
    c_sum.scatter()
    g_sum.gather()
    c_sum.cross()
    g_sum.finish()
    c_sum.gather()

    def whole(total, rows):
        tiles_of = total[...].reshape(rows // 4, 8, 128)
        return jnp.concatenate(
            [
                jnp.concatenate([tiles_of[2 * at], tiles_of[2 * at + 1]], axis=1)
                for at in range(rows // 8)
            ],
            axis=0,
        )

    eye = jnp.where(
        lanes_of((kept, 256)) == lax.broadcasted_iota(jnp.int32, (kept, 256), 0), 1.0, 0.0
    ).astype(F32)
    h_one = jnp.concatenate(
        [eye - whole(g_result, kept) * scale, jnp.zeros((256 - kept, 256), F32)], axis=0
    )
    h_two = dot_full(h_one, h_one, NN)
    h_sum = h_one + h_two + dot_full(h_one, h_two, NN)
    h_high, h_low = split(jnp.concatenate([h_one, h_sum], axis=1))

    c_sum.finish()
    c_full = whole(c_result, columns) * scale
    lane = lanes_of((columns, 256))
    c_one = jnp.where(lane < kept, c_full, 0.0)
    square = c_full[:, kept : kept + columns]
    c_both = jnp.concatenate(split(c_one), axis=0)
    moved = dot(c_both, h_high, NN) + dot(c_both, h_low, NN)
    moved = moved[0:columns] + moved[columns:]
    total = c_one + moved[:, 0:256]
    gram = square - dot_full(c_one + moved[:, 256:], c_one, NT)
    proj[...] = total[:, 0:kept]

    p_high, p_low = split(total)
    p_both = jnp.concatenate([p_high, p_low], axis=0)[:, 0:kept]
    for at in range(0, cells, chunk):
        here = slice(at, at + chunk)
        part = dot(p_both, high[0:kept, here], NN) + dot(p_both, low[0:kept, here], NN)
        residual[:, here] = flat_image[:, here] - part[0:columns] - part[columns:]

    wide = (columns, 128)
    lane = lanes_of(wide)
    row = lax.broadcasted_iota(jnp.int32, wide, 0)
    table = jnp.where(lane == row + columns, 1.0, 0.0).astype(F32)
    table = table + jnp.concatenate([gram, jnp.zeros((columns, 128 - columns), F32)], axis=1)
    step = 8
    for first in range(0, columns, step):
        ahead = [
            jnp.broadcast_to(table[:, first + j : first + j + 1], wide) for j in range(step)
        ]
        for j in range(step):
            k = first + j
            root = lax.rsqrt(ahead[j][k : k + 1, :])
            column = ahead[j] * root
            line = table[k : k + 1, :] * root
            chol[k : k + 1, :] = line
            table = table - column * line
            for m in range(j + 1, step):
                ahead[m] = ahead[m] - column * column[first + m : first + m + 1, :]
    done = chol[...]
    factor[...] = jnp.where(lane >= row, done, 0.0)[:, 0:columns]
    inverse = jnp.concatenate(split(done[:, columns : 2 * columns]), axis=0)
    copies = []
    for x in range(span):
        here = slice(x * 1024, x * 1024 + 1024)
        one, two = split(residual[:, here])
        part = dot(inverse, one, NN) + dot(inverse, two, NN)
        part = part[0:columns] + part[columns:]
        for k in range(8):
            image_rows[pl.ds(x * 8 + k, columns, stride=plane), :] = part[:, 128 * k : 128 * k + 128]
        copies.append(pltpu.make_async_copy(image.at[:, x], out.at[:, x], out_sems.at[x]))
        copies[-1].start()
    for copy in copies:
        copy.wait()

    rim1.drain()
    rim2.drain()
    g_sum.drain()
    c_sum.drain()


def hand_over_kernel(*refs):
    sems = refs[6]
    copies = [pltpu.make_async_copy(refs[i], refs[3 + i], sems.at[i]) for i in range(3)]
    for copy in copies:
        copy.start()
    for copy in copies:
        copy.wait()


def hand_over(*arrays):
    return pl.pallas_call(
        hand_over_kernel,
        out_shape=tuple(jax.ShapeDtypeStruct(a.shape, a.dtype) for a in arrays),
        in_specs=[pl.BlockSpec(memory_space=pl.ANY)] * 3,
        out_specs=tuple([pl.BlockSpec(memory_space=pl.ANY)] * 3),
        scratch_shapes=[pltpu.SemaphoreType.DMA((3,))],
        compiler_params=pltpu.CompilerParams(vmem_limit_bytes=VMEM_GRANT),
        name="hand_over",
    )(*arrays)


def shards(sizes, noise, basis, cond, react):
    columns, span, rows, lanes = noise.shape
    kept = basis.shape[0]
    plane = span * rows
    cells = plane * lanes
    cell_total = float(cells * sizes["gx"] * sizes["gy"] * sizes["gz"])
    c_tiles, g_tiles = columns // 4, kept // 4
    own, rest, count = [], [], 1
    for axis in ("gx", "gy", "gz"):
        if c_tiles % (count * sizes[axis]) == 0:
            count *= sizes[axis]
            own.append(axis)
        else:
            rest.append(axis)
    owners, others = Team(own, sizes), Team(rest, sizes)
    vmem = lambda *shape: pltpu.VMEM(shape, F32)
    y_rows = -(-(columns + 1) * span // 8) * 8

    def sum_buffers(tiles):
        share = tiles // owners.count
        return [
            vmem(tiles, 8, 128),
            vmem(owners.count, share, 8, 128),
            vmem(others.count, share, 8, 128),
            vmem(owners.count, share, 8, 128),
        ]

    dma = lambda n: pltpu.SemaphoreType.DMA((n,))
    sum_sems = [dma(n) for n in (owners.count, owners.count, others.count, others.count, owners.count, owners.count)]
    scratch = [
        vmem(columns + 1, span, 8, 128),
        vmem(columns, span, 8, 128),
        vmem(columns, span, 8, 128),
        vmem(kept * plane, 128),
        vmem(span, 8, 128),
        vmem(7, span, 8, 128),
        pltpu.VMEM((256, cells), BF16),
        pltpu.VMEM((256, cells), BF16),
        vmem(columns, cells),
        vmem(columns, cells),
        vmem(columns, 128),
        vmem(2, columns + 1, 8, 128),
        vmem(2, columns, 8, 128),
        vmem(2, y_rows, 128),
        vmem(2, y_rows, 128),
        vmem(2, columns * span, 128),
        vmem(2, columns * span, 128),
        vmem(2, 2, 8, 128),
        vmem(2, 2, 8, 128),
        vmem(2, 1, 8, 128),
        vmem(2, 1, 8, 128),
        *sum_buffers(c_tiles),
        *sum_buffers(g_tiles),
        dma(4),
        dma(span),
        dma(6),
        dma(6),
        dma(6),
        dma(6),
        *sum_sems,
        *sum_sems,
    ]
    out, factor, proj = pl.pallas_call(
        functools.partial(kernel, sizes, owners, others, cell_total),
        out_shape=(
            jax.ShapeDtypeStruct(noise.shape, F32),
            jax.ShapeDtypeStruct((columns, columns), F32),
            jax.ShapeDtypeStruct((columns, kept), F32),
        ),
        in_specs=[pl.BlockSpec(memory_space=pl.ANY)] * 4,
        out_specs=(
            pl.BlockSpec(memory_space=pl.ANY),
            pl.BlockSpec(memory_space=pltpu.VMEM),
            pl.BlockSpec(memory_space=pltpu.VMEM),
        ),
        scratch_shapes=scratch,
        compiler_params=pltpu.CompilerParams(
            collective_id=0, has_side_effects=True, vmem_limit_bytes=VMEM_GRANT
        ),
        name="lanczos_step",
    )(noise, basis.reshape(kept * plane, lanes), cond, react)
    out, factor, proj = hand_over(out, factor, proj)
    return out, factor, proj.T


def solution(mesh):
    sizes = dict(mesh.shape)
    return jax.shard_map(
        functools.partial(shards, sizes),
        mesh=mesh,
        in_specs=(
            P(None, "gx", "gy", "gz"),
            P(None, "gx", "gy", "gz"),
            P("gx", "gy", "gz"),
            P("gx", "gy", "gz"),
        ),
        out_specs=(P(None, "gx", "gy", "gz"), P(), P()),
        check_vma=False,
    )
```

```python
import functools

import jax
import jax.numpy as jnp
from jax import lax
from jax.experimental import pallas as pl
from jax.experimental.pallas import tpu as pltpu
from jax.sharding import PartitionSpec as P

MESH = pl.DeviceIdType.MESH
GROUP = 8
VMEM_GRANT = 63 * 1024 * 1024
F32 = jnp.float32
BF16 = jnp.bfloat16


def each(count, body):
    if count <= 8:
        for k in range(1, count):
            body(k)
    else:
        lax.fori_loop(1, count, lambda k, c: (body(k), c)[1], 0)


class Team:
    def __init__(self, axes, sizes):
        self.axes = axes
        self.sizes = sizes
        self.count = 1
        for axis in axes:
            self.count *= sizes[axis]

    def me(self):
        index = 0
        for axis in self.axes:
            index = index * self.sizes[axis] + lax.axis_index(axis)
        return index

    def device(self, index):
        out = {}
        for axis in reversed(self.axes):
            out[axis] = lax.rem(index, self.sizes[axis])
            index = lax.div(index, self.sizes[axis])
        return out

    def peer(self, k):
        return lax.rem(self.me() + k, self.count)


class Sum:
    def __init__(self, owners, others, data, landed, crossed, result, sems):
        self.owners, self.others = owners, others
        self.data, self.landed, self.crossed, self.result = data, landed, crossed, result
        self.sems = sems
        self.share = data.shape[0] // owners.count

    def copy(self, phase, team, src, dst_ref, slot, peer):
        send, recv = self.sems[2 * phase], self.sems[2 * phase + 1]
        return pltpu.make_async_remote_copy(
            src_ref=src,
            dst_ref=dst_ref.at[slot],
            send_sem=send.at[peer],
            recv_sem=recv.at[slot],
            device_id=team.device(peer),
            device_id_type=MESH,
        )

    def piece(self, index):
        return self.data.at[pl.ds(index * self.share, self.share)]

    def scatter(self):
        team, me = self.owners, self.owners.me()

        def go(k):
            peer = team.peer(k)
            self.copy(0, team, self.piece(peer), self.landed, me, peer).start()

        each(team.count, go)
        self.landed[me] = self.data[pl.ds(me * self.share, self.share)]

    def settle(self, phase, team, src, dst_ref):
        def go(k):
            peer = team.peer(k)
            self.copy(phase, team, src, dst_ref, peer, peer).wait_recv()

        each(team.count, go)

    def cross(self):
        self.settle(0, self.owners, self.piece(0), self.landed)
        team, me = self.others, self.others.me()
        total = self.landed[0]
        for k in range(1, self.owners.count):
            total = total + self.landed[k]
        self.crossed[me] = total

        def go(k):
            peer = team.peer(k)
            self.copy(1, team, self.crossed.at[me], self.crossed, me, peer).start()

        each(team.count, go)

    def gather(self):
        self.settle(1, self.others, self.crossed.at[0], self.crossed)
        team, me = self.owners, self.owners.me()
        total = self.crossed[0]
        for k in range(1, self.others.count):
            total = total + self.crossed[k]
        self.result[me] = total

        def go(k):
            peer = team.peer(k)
            self.copy(2, team, self.result.at[me], self.result, me, peer).start()

        each(team.count, go)

    def finish(self):
        self.settle(2, self.owners, self.result.at[0], self.result)

    def drain(self):
        def scattered(k):
            peer = self.owners.peer(k)
            self.copy(0, self.owners, self.piece(0), self.landed, 0, peer).wait_send()

        def crossed(k):
            peer = self.others.peer(k)
            self.copy(1, self.others, self.crossed.at[0], self.crossed, 0, peer).wait_send()

        def gathered(k):
            peer = self.owners.peer(k)
            self.copy(2, self.owners, self.result.at[0], self.result, 0, peer).wait_send()

        each(self.owners.count, scattered)
        each(self.others.count, crossed)
        each(self.owners.count, gathered)


class Rim:
    def __init__(self, field, x_in, y_out, y_in, z_out, z_in, send, recv, sizes):
        self.sizes = sizes
        self.send, self.recv = send, recv
        last = field.shape[1] - 1
        self.routes = (
            ("gx", (field.at[:, 0], field.at[:, last]), x_in),
            ("gy", (y_out.at[0], y_out.at[1]), y_in),
            ("gz", (z_out.at[0], z_out.at[1]), z_in),
        )

    def exists(self, axis, side):
        me = lax.axis_index(axis)
        return me > 0 if side == 0 else me < self.sizes[axis] - 1

    def copy(self, at, side):
        axis, out, into = self.routes[at]
        me = lax.axis_index(axis)
        step = -1 if side == 0 else 1
        return pltpu.make_async_remote_copy(
            src_ref=out[side],
            dst_ref=into.at[1 - side],
            send_sem=self.send.at[2 * at + side],
            recv_sem=self.recv.at[2 * at + 1 - side],
            device_id={axis: me + step},
            device_id_type=MESH,
        )

    def start(self, at):
        axis = self.routes[at][0]
        for side in range(2):
            pl.when(self.exists(axis, side))(lambda at=at, side=side: self.copy(at, side).start())

    def blank(self):
        for axis, _, into in self.routes:
            for side in range(2):
                @pl.when(jnp.logical_not(self.exists(axis, side)))
                def _(into=into, side=side):
                    into[side] = jnp.zeros(into.shape[1:], F32)

    def arrive(self):
        for at in range(3):
            axis = self.routes[at][0]
            for side in range(2):
                pl.when(self.exists(axis, side))(
                    lambda at=at, side=side: self.copy(at, 1 - side).wait_recv()
                )

    def drain(self):
        for at in range(3):
            axis = self.routes[at][0]
            for side in range(2):
                pl.when(self.exists(axis, side))(
                    lambda at=at, side=side: self.copy(at, side).wait_send()
                )


def lanes_of(shape):
    return lax.broadcasted_iota(jnp.int32, shape, len(shape) - 1)


def pack_y(flat, rows, y_out):
    for side, first in ((0, 0), (1, 7)):
        y_out[side, pl.ds(0, rows), :] = flat[pl.ds(first, rows, stride=8), :]


def pack_z(tiles, lanes_total):
    lane = lanes_of((8, 128))
    lo = jnp.zeros((8, 128), F32)
    hi = jnp.zeros((8, 128), F32)
    for i in range(lanes_total):
        tile = tiles[i]
        lo = jnp.where(lane == i, jnp.broadcast_to(tile[:, 0:1], (8, 128)), lo)
        hi = jnp.where(lane == i, jnp.broadcast_to(tile[:, 127:128], (8, 128)), hi)
    return lo, hi


def neighbours(value, x_lo, x_hi, y_lo, y_hi, z_lo, z_hi):
    count, span = value.shape[0], value.shape[1]
    tiles = count * span
    flat = value.reshape(tiles, 8, 128)
    below = jnp.concatenate([x_lo[:, None], value[:, : span - 1]], axis=1)
    above = jnp.concatenate([value[:, 1:], x_hi[:, None]], axis=1)
    row = lax.broadcasted_iota(jnp.int32, (8, 128), 0)
    lane = lanes_of((8, 128))
    before, after, left, right = [], [], [], []
    for i in range(tiles):
        tile = flat[i]
        before.append(
            jnp.where(row == 0, jnp.broadcast_to(y_lo[i], (8, 128)), pltpu.roll(tile, 1, 0))
        )
        after.append(
            jnp.where(row == 7, jnp.broadcast_to(y_hi[i], (8, 128)), pltpu.roll(tile, 7, 0))
        )
        left.append(
            jnp.where(lane == 0, jnp.broadcast_to(z_lo[:, i : i + 1], (8, 128)), pltpu.roll(tile, 1, 1))
        )
        right.append(
            jnp.where(
                lane == 127, jnp.broadcast_to(z_hi[:, i : i + 1], (8, 128)), pltpu.roll(tile, 127, 1)
            )
        )
    join = lambda parts: jnp.stack(parts).reshape(value.shape)
    return above, below, join(after), join(before), join(right), join(left)


def split(value):
    high = value.astype(BF16)
    return high, (value - high.astype(F32)).astype(BF16)


def dot(left, right, dims):
    return lax.dot_general(left, right, (dims, ((), ())), preferred_element_type=F32)


def dot_full(left, right, dims):
    return lax.dot_general(
        left, right, (dims, ((), ())), precision=lax.Precision.HIGHEST, preferred_element_type=F32
    )


NT = ((1,), (1,))
NN = ((1,), (0,))


def kernel(sizes, owners, others, cell_total, noise, basis, cond, react, left_over, chol, proj, *scratch):
    (field, field2, image, stored, react_v, coef, high, low, flat_image, residual,
     x_in1, x_in2, y_out1, y_in1, y_out2, y_in2, z_out1, z_in1, z_out2, z_in2,
     c_data, c_landed, c_crossed, c_result, g_data, g_landed, g_crossed, g_result,
     in_sems, out_sems, h_send1, h_recv1, h_send2, h_recv2, *sum_sems) = scratch
    columns, span = field2.shape[0], field2.shape[1]
    plane = span * 8
    kept = basis.shape[0] // plane
    cells = plane * 128
    tiles = columns * span
    scale = 1.0 / cell_total

    load_noise = pltpu.make_async_copy(noise, field.at[pl.ds(0, columns)], in_sems.at[0])
    load_cond = pltpu.make_async_copy(cond, field.at[columns], in_sems.at[1])
    load_react = pltpu.make_async_copy(react, react_v, in_sems.at[2])
    load_basis = pltpu.make_async_copy(basis, stored, in_sems.at[3])
    load_noise.start()
    load_cond.start()
    load_react.start()
    load_basis.start()

    barrier = pltpu.get_barrier_semaphore()
    for team in (owners, others):
        def greet(k, team=team):
            pl.semaphore_signal(
                barrier, inc=1, device_id=team.device(team.peer(k)), device_id_type=MESH
            )
        each(team.count, greet)

    rim1 = Rim(field, x_in1, y_out1, y_in1, z_out1, z_in1, h_send1, h_recv1, sizes)
    rim2 = Rim(field2, x_in2, y_out2, y_in2, z_out2, z_in2, h_send2, h_recv2, sizes)
    rim1.blank()
    rim2.blank()
    load_noise.wait()
    load_cond.wait()
    pl.semaphore_wait(barrier, owners.count + others.count - 2)
    rim1.start(0)
    field_flat = field.reshape((columns + 1) * plane, 128)
    y_rows = tiles + span
    y_out1[...] = jnp.zeros(y_out1.shape, F32)
    pack_y(field_flat, y_rows, y_out1)
    rim1.start(1)
    lo, hi = pack_z(field[0:columns].reshape(tiles, 8, 128), tiles)
    z_out1[0, 0], z_out1[1, 0] = lo, hi
    lo, hi = pack_z(field[columns], span)
    z_out1[0, 1], z_out1[1, 1] = lo, hi
    rim1.start(2)

    load_basis.wait()
    spare = high.shape[0] - kept
    high[kept:, :] = jnp.zeros((spare, cells), BF16)
    low[kept:, :] = jnp.zeros((spare, cells), BF16)
    for at in range(plane):
        one, two = split(stored[pl.ds(at, kept, stride=plane), :])
        high[0:kept, at * 128 : (at + 1) * 128] = one
        low[0:kept, at * 128 : (at + 1) * 128] = two

    load_react.wait()
    rim1.arrive()
    theta = field[columns]
    around = neighbours(
        theta[None],
        x_in1[0, columns][None],
        x_in1[1, columns][None],
        [y_in1[0, pl.ds(tiles + i, 1), :] for i in range(span)],
        [y_in1[1, pl.ds(tiles + i, 1), :] for i in range(span)],
        z_in1[0, 1],
        z_in1[1, 1],
    )
    diagonal = react_v[...]
    for face, other in enumerate(around):
        value = 0.5 * (theta + other[0])
        coef[face] = value
        diagonal = diagonal + value
    coef[6] = diagonal

    def apply(source, x_in, y_in, z_in, group):
        start = group * GROUP
        value = source[pl.ds(start, GROUP)]
        shift = (128 - group * (GROUP * span)) % 128
        first = start * span
        around = neighbours(
            value,
            x_in[0, pl.ds(start, GROUP)],
            x_in[1, pl.ds(start, GROUP)],
            [y_in[0, pl.ds(first + i, 1), :] for i in range(GROUP * span)],
            [y_in[1, pl.ds(first + i, 1), :] for i in range(GROUP * span)],
            pltpu.roll(z_in[0, 0], shift, 1) if shift else z_in[0, 0],
            pltpu.roll(z_in[1, 0], shift, 1) if shift else z_in[1, 0],
        )
        result = react_v[...][None] * value
        for face, other in enumerate(around):
            result = result + coef[face][None] * (value - other)
        return start, result

    def first_step(group):
        start, result = apply(field, x_in1, y_in1, z_in1, group)
        field2[pl.ds(start, GROUP)] = result / coef[6][None]

    for group in range(columns // GROUP):
        first_step(group)
    rim2.start(0)
    pack_y(field2.reshape(columns * plane, 128), tiles, y_out2)
    rim2.start(1)
    lo, hi = pack_z(field2[...].reshape(tiles, 8, 128), tiles)
    z_out2[0, 0], z_out2[1, 0] = lo, hi
    rim2.start(2)

    chunk = 1024
    g_one = jnp.zeros((kept, 256), F32)
    g_two = jnp.zeros((kept, 256), F32)
    for at in range(0, cells, chunk):
        right = high[:, at : at + chunk]
        g_one = g_one + dot(high[0:kept, at : at + chunk], right, NT)
        g_two = g_two + dot(low[0:kept, at : at + chunk], right, NT)
    turned = jnp.transpose(jnp.concatenate([g_two, jnp.zeros((256 - kept, 256), F32)], axis=0))
    g_local = g_one + g_two + turned[0:kept]
    for at in range(kept // 8):
        for half in range(2):
            g_data[2 * at + half] = g_local[8 * at : 8 * at + 8, 128 * half : 128 * half + 128]

    c_sum = Sum(owners, others, c_data, c_landed, c_crossed, c_result, sum_sems[0:6])
    g_sum = Sum(owners, others, g_data, g_landed, g_crossed, g_result, sum_sems[6:12])
    g_sum.scatter()

    rim2.arrive()

    def second_step(group):
        start, result = apply(field2, x_in2, y_in2, z_in2, group)
        image[pl.ds(start, GROUP)] = result

    for group in range(columns // GROUP):
        second_step(group)
    image_rows = image.reshape(columns * plane, 128)
    for at in range(plane):
        value = image_rows[pl.ds(at, columns, stride=plane), :]
        flat_image[:, at * 128 : (at + 1) * 128] = value
        one, two = split(value)
        high[kept : kept + columns, at * 128 : (at + 1) * 128] = one
        low[kept : kept + columns, at * 128 : (at + 1) * 128] = two

    both = jnp.zeros((2 * columns, 256), F32)
    for at in range(0, cells, chunk):
        here = slice(at, at + chunk)
        left = jnp.concatenate([high[kept : kept + columns, here], low[kept : kept + columns, here]], axis=0)
        both = both + dot(left, high[:, here], NT) + dot(left, low[:, here], NT)
    c_local = both[0:columns] + both[columns:]
    for at in range(columns // 8):
        for half in range(2):
            c_data[2 * at + half] = c_local[8 * at : 8 * at + 8, 128 * half : 128 * half + 128]
    g_sum.cross()
    c_sum.scatter()
    g_sum.gather()
    c_sum.cross()
    g_sum.finish()
    c_sum.gather()

    def whole(total, rows):
        tiles_of = total[...].reshape(rows // 4, 8, 128)
        return jnp.concatenate(
            [
                jnp.concatenate([tiles_of[2 * at], tiles_of[2 * at + 1]], axis=1)
                for at in range(rows // 8)
            ],
            axis=0,
        )

    eye = jnp.where(
        lanes_of((kept, 256)) == lax.broadcasted_iota(jnp.int32, (kept, 256), 0), 1.0, 0.0
    ).astype(F32)
    h_one = jnp.concatenate(
        [eye - whole(g_result, kept) * scale, jnp.zeros((256 - kept, 256), F32)], axis=0
    )
    h_two = dot_full(h_one, h_one, NN)
    h_sum = h_one + h_two + dot_full(h_one, h_two, NN)
    h_high, h_low = split(jnp.concatenate([h_one, h_sum], axis=1))

    c_sum.finish()
    c_full = whole(c_result, columns) * scale
    lane = lanes_of((columns, 256))
    c_one = jnp.where(lane < kept, c_full, 0.0)
    square = c_full[:, kept : kept + columns]
    c_both = jnp.concatenate(split(c_one), axis=0)
    moved = dot(c_both, h_high, NN) + dot(c_both, h_low, NN)
    moved = moved[0:columns] + moved[columns:]
    total = c_one + moved[:, 0:256]
    gram = square - dot_full(c_one + moved[:, 256:], c_one, NT)
    proj[...] = total[:, 0:kept]

    p_high, p_low = split(total)
    p_both = jnp.concatenate([p_high, p_low], axis=0)[:, 0:kept]
    for at in range(0, cells, chunk):
        here = slice(at, at + chunk)
        part = dot(p_both, high[0:kept, here], NN) + dot(p_both, low[0:kept, here], NN)
        residual[:, here] = flat_image[:, here] - part[0:columns] - part[columns:]
    write = pltpu.make_async_copy(residual, left_over, out_sems.at[0])
    write.start()

    wide = (columns, 128)
    lane = lanes_of(wide)
    row = lax.broadcasted_iota(jnp.int32, wide, 0)
    table = jnp.where(lane == row + columns, 1.0, 0.0).astype(F32)
    table = table + jnp.concatenate([gram, jnp.zeros((columns, 128 - columns), F32)], axis=1)
    step = 8
    for first in range(0, columns, step):
        ahead = [
            jnp.broadcast_to(table[:, first + j : first + j + 1], wide) for j in range(step)
        ]
        for j in range(step):
            k = first + j
            root = lax.rsqrt(ahead[j][k : k + 1, :])
            column = ahead[j] * root
            line = table[k : k + 1, :] * root
            chol[k : k + 1, :] = line
            table = table - column * line
            for m in range(j + 1, step):
                ahead[m] = ahead[m] - column * column[first + m : first + m + 1, :]
    write.wait()
    rim1.drain()
    rim2.drain()
    g_sum.drain()
    c_sum.drain()


def finish_kernel(left_over, chol, proj, out, factor, proj_out, rest, table, kept, upper, new, sems):
    columns, span = new.shape[0], new.shape[1]
    width = rest.shape[1] // span
    load_table = pltpu.make_async_copy(chol, table, sems.at[0])
    load_proj = pltpu.make_async_copy(proj, kept, sems.at[1])
    loads = [
        pltpu.make_async_copy(
            left_over.at[:, pl.ds(x * width, width)], rest.at[:, pl.ds(x * width, width)], sems.at[4 + x]
        )
        for x in range(span)
    ]
    load_table.start()
    for load in loads:
        load.start()
    load_proj.start()
    load_table.wait()
    done = table[...]
    row = lax.broadcasted_iota(jnp.int32, done.shape, 0)
    upper[...] = jnp.where(lanes_of(done.shape) >= row, done, 0.0)[:, 0:columns]
    store_factor = pltpu.make_async_copy(upper, factor, sems.at[2])
    store_factor.start()
    load_proj.wait()
    store_proj = pltpu.make_async_copy(kept, proj_out, sems.at[3])
    store_proj.start()
    inverse = jnp.concatenate(split(done[:, columns : 2 * columns]), axis=0)
    rows = new.reshape(columns * span * 8, 128)
    stores = []
    for x in range(span):
        loads[x].wait()
        one, two = split(rest[:, x * width : (x + 1) * width])
        part = dot(inverse, one, NN) + dot(inverse, two, NN)
        part = part[0:columns] + part[columns:]
        for k in range(8):
            rows[pl.ds(x * 8 + k, columns, stride=span * 8), :] = part[:, 128 * k : 128 * k + 128]
        stores.append(pltpu.make_async_copy(new.at[:, x], out.at[:, x], sems.at[4 + span + x]))
        stores[-1].start()
    for store in stores:
        store.wait()
    store_factor.wait()
    store_proj.wait()


def finish(left_over, chol, proj, shape):
    columns, span = shape[0], shape[1]
    return pl.pallas_call(
        finish_kernel,
        out_shape=(
            jax.ShapeDtypeStruct(shape, F32),
            jax.ShapeDtypeStruct((columns, columns), F32),
            jax.ShapeDtypeStruct(proj.shape, F32),
        ),
        in_specs=[pl.BlockSpec(memory_space=pl.ANY)] * 3,
        out_specs=tuple([pl.BlockSpec(memory_space=pl.ANY)] * 3),
        scratch_shapes=[
            pltpu.VMEM(left_over.shape, F32),
            pltpu.VMEM(chol.shape, F32),
            pltpu.VMEM(proj.shape, F32),
            pltpu.VMEM((columns, columns), F32),
            pltpu.VMEM(shape, F32),
            pltpu.SemaphoreType.DMA((4 + 2 * span,)),
        ],
        compiler_params=pltpu.CompilerParams(vmem_limit_bytes=VMEM_GRANT),
        name="new_block",
    )(left_over, chol, proj)


def shards(sizes, noise, basis, cond, react):
    columns, span, rows, lanes = noise.shape
    kept = basis.shape[0]
    plane = span * rows
    cells = plane * lanes
    cell_total = float(cells * sizes["gx"] * sizes["gy"] * sizes["gz"])
    c_tiles, g_tiles = columns // 4, kept // 4
    own, rest, count = [], [], 1
    for axis in ("gx", "gy", "gz"):
        if c_tiles % (count * sizes[axis]) == 0:
            count *= sizes[axis]
            own.append(axis)
        else:
            rest.append(axis)
    owners, others = Team(own, sizes), Team(rest, sizes)
    vmem = lambda *shape: pltpu.VMEM(shape, F32)
    y_rows = -(-(columns + 1) * span // 8) * 8

    def sum_buffers(tiles):
        share = tiles // owners.count
        return [
            vmem(tiles, 8, 128),
            vmem(owners.count, share, 8, 128),
            vmem(others.count, share, 8, 128),
            vmem(owners.count, share, 8, 128),
        ]

    dma = lambda n: pltpu.SemaphoreType.DMA((n,))
    sum_sems = [dma(n) for n in (owners.count, owners.count, others.count, others.count, owners.count, owners.count)]
    scratch = [
        vmem(columns + 1, span, 8, 128),
        vmem(columns, span, 8, 128),
        vmem(columns, span, 8, 128),
        vmem(kept * plane, 128),
        vmem(span, 8, 128),
        vmem(7, span, 8, 128),
        pltpu.VMEM((256, cells), BF16),
        pltpu.VMEM((256, cells), BF16),
        vmem(columns, cells),
        vmem(columns, cells),
        vmem(2, columns + 1, 8, 128),
        vmem(2, columns, 8, 128),
        vmem(2, y_rows, 128),
        vmem(2, y_rows, 128),
        vmem(2, columns * span, 128),
        vmem(2, columns * span, 128),
        vmem(2, 2, 8, 128),
        vmem(2, 2, 8, 128),
        vmem(2, 1, 8, 128),
        vmem(2, 1, 8, 128),
        *sum_buffers(c_tiles),
        *sum_buffers(g_tiles),
        dma(4),
        dma(1),
        dma(6),
        dma(6),
        dma(6),
        dma(6),
        *sum_sems,
        *sum_sems,
    ]
    left_over, chol, proj = pl.pallas_call(
        functools.partial(kernel, sizes, owners, others, cell_total),
        out_shape=(
            jax.ShapeDtypeStruct((columns, cells), F32),
            jax.ShapeDtypeStruct((columns, 128), F32),
            jax.ShapeDtypeStruct((columns, kept), F32),
        ),
        in_specs=[pl.BlockSpec(memory_space=pl.ANY)] * 4,
        out_specs=(
            pl.BlockSpec(memory_space=pl.ANY),
            pl.BlockSpec(memory_space=pltpu.VMEM),
            pl.BlockSpec(memory_space=pltpu.VMEM),
        ),
        scratch_shapes=scratch,
        compiler_params=pltpu.CompilerParams(
            collective_id=0, has_side_effects=True, vmem_limit_bytes=VMEM_GRANT
        ),
        name="lanczos_step",
    )(noise, basis.reshape(kept * plane, lanes), cond, react)
    out, factor, proj = finish(left_over, chol, proj, noise.shape)
    return out, factor, proj.T


def solution(mesh):
    sizes = dict(mesh.shape)
    return jax.shard_map(
        functools.partial(shards, sizes),
        mesh=mesh,
        in_specs=(
            P(None, "gx", "gy", "gz"),
            P(None, "gx", "gy", "gz"),
            P("gx", "gy", "gz"),
            P("gx", "gy", "gz"),
        ),
        out_specs=(P(None, "gx", "gy", "gz"), P(), P()),
        check_vma=False,
    )
```

```python
import functools

import jax
import jax.numpy as jnp
from jax import lax
from jax.experimental import pallas as pl
from jax.experimental.pallas import tpu as pltpu
from jax.sharding import PartitionSpec as P

MESH = pl.DeviceIdType.MESH
GROUP = 8
VMEM_GRANT = 63 * 1024 * 1024
F32 = jnp.float32
BF16 = jnp.bfloat16


def each(count, body):
    if count <= 8:
        for k in range(1, count):
            body(k)
    else:
        lax.fori_loop(1, count, lambda k, c: (body(k), c)[1], 0)


class Team:
    def __init__(self, axes, sizes):
        self.axes = axes
        self.sizes = sizes
        self.count = 1
        for axis in axes:
            self.count *= sizes[axis]

    def me(self):
        index = 0
        for axis in self.axes:
            index = index * self.sizes[axis] + lax.axis_index(axis)
        return index

    def device(self, index):
        out = {}
        for axis in reversed(self.axes):
            out[axis] = lax.rem(index, self.sizes[axis])
            index = lax.div(index, self.sizes[axis])
        return out

    def peer(self, k):
        return lax.rem(self.me() + k, self.count)


class Sum:
    def __init__(self, owners, others, data, landed, crossed, result, sems):
        self.owners, self.others = owners, others
        self.data, self.landed, self.crossed, self.result = data, landed, crossed, result
        self.sems = sems
        self.share = data.shape[0] // owners.count

    def copy(self, phase, team, src, dst_ref, slot, peer):
        send, recv = self.sems[2 * phase], self.sems[2 * phase + 1]
        return pltpu.make_async_remote_copy(
            src_ref=src,
            dst_ref=dst_ref.at[slot],
            send_sem=send.at[peer],
            recv_sem=recv.at[slot],
            device_id=team.device(peer),
            device_id_type=MESH,
        )

    def piece(self, index):
        return self.data.at[pl.ds(index * self.share, self.share)]

    def scatter(self):
        team, me = self.owners, self.owners.me()

        def go(k):
            peer = team.peer(k)
            self.copy(0, team, self.piece(peer), self.landed, me, peer).start()

        each(team.count, go)
        self.landed[me] = self.data[pl.ds(me * self.share, self.share)]

    def settle(self, phase, team, src, dst_ref):
        def go(k):
            peer = team.peer(k)
            self.copy(phase, team, src, dst_ref, peer, peer).wait_recv()

        each(team.count, go)

    def cross(self):
        self.settle(0, self.owners, self.piece(0), self.landed)
        team, me = self.others, self.others.me()
        total = self.landed[0]
        for k in range(1, self.owners.count):
            total = total + self.landed[k]
        self.crossed[me] = total

        def go(k):
            peer = team.peer(k)
            self.copy(1, team, self.crossed.at[me], self.crossed, me, peer).start()

        each(team.count, go)

    def gather(self):
        self.settle(1, self.others, self.crossed.at[0], self.crossed)
        team, me = self.owners, self.owners.me()
        total = self.crossed[0]
        for k in range(1, self.others.count):
            total = total + self.crossed[k]
        self.result[me] = total

        def go(k):
            peer = team.peer(k)
            self.copy(2, team, self.result.at[me], self.result, me, peer).start()

        each(team.count, go)

    def finish(self):
        self.settle(2, self.owners, self.result.at[0], self.result)

    def drain(self):
        def scattered(k):
            peer = self.owners.peer(k)
            self.copy(0, self.owners, self.piece(0), self.landed, 0, peer).wait_send()

        def crossed(k):
            peer = self.others.peer(k)
            self.copy(1, self.others, self.crossed.at[0], self.crossed, 0, peer).wait_send()

        def gathered(k):
            peer = self.owners.peer(k)
            self.copy(2, self.owners, self.result.at[0], self.result, 0, peer).wait_send()

        each(self.owners.count, scattered)
        each(self.others.count, crossed)
        each(self.owners.count, gathered)


class Rim:
    def __init__(self, field, x_in, y_out, y_in, z_out, z_in, send, recv, sizes):
        self.sizes = sizes
        self.send, self.recv = send, recv
        last = field.shape[1] - 1
        self.routes = (
            ("gx", (field.at[:, 0], field.at[:, last]), x_in),
            ("gy", (y_out.at[0], y_out.at[1]), y_in),
            ("gz", (z_out.at[0], z_out.at[1]), z_in),
        )

    def exists(self, axis, side):
        me = lax.axis_index(axis)
        return me > 0 if side == 0 else me < self.sizes[axis] - 1

    def copy(self, at, side):
        axis, out, into = self.routes[at]
        me = lax.axis_index(axis)
        step = -1 if side == 0 else 1
        return pltpu.make_async_remote_copy(
            src_ref=out[side],
            dst_ref=into.at[1 - side],
            send_sem=self.send.at[2 * at + side],
            recv_sem=self.recv.at[2 * at + 1 - side],
            device_id={axis: me + step},
            device_id_type=MESH,
        )

    def start(self, at):
        axis = self.routes[at][0]
        for side in range(2):
            pl.when(self.exists(axis, side))(lambda at=at, side=side: self.copy(at, side).start())

    def blank(self):
        for axis, _, into in self.routes:
            for side in range(2):
                @pl.when(jnp.logical_not(self.exists(axis, side)))
                def _(into=into, side=side):
                    into[side] = jnp.zeros(into.shape[1:], F32)

    def arrive(self):
        for at in range(3):
            axis = self.routes[at][0]
            for side in range(2):
                pl.when(self.exists(axis, side))(
                    lambda at=at, side=side: self.copy(at, 1 - side).wait_recv()
                )

    def drain(self):
        for at in range(3):
            axis = self.routes[at][0]
            for side in range(2):
                pl.when(self.exists(axis, side))(
                    lambda at=at, side=side: self.copy(at, side).wait_send()
                )


def lanes_of(shape):
    return lax.broadcasted_iota(jnp.int32, shape, len(shape) - 1)


def pack_y(flat, rows, y_out):
    for side, first in ((0, 0), (1, 7)):
        y_out[side, pl.ds(0, rows), :] = flat[pl.ds(first, rows, stride=8), :]


def pack_z(tiles, lanes_total):
    lane = lanes_of((8, 128))
    lo = jnp.zeros((8, 128), F32)
    hi = jnp.zeros((8, 128), F32)
    for i in range(lanes_total):
        tile = tiles[i]
        lo = jnp.where(lane == i, jnp.broadcast_to(tile[:, 0:1], (8, 128)), lo)
        hi = jnp.where(lane == i, jnp.broadcast_to(tile[:, 127:128], (8, 128)), hi)
    return lo, hi


def neighbours(value, x_lo, x_hi, y_lo, y_hi, z_lo, z_hi):
    count, span = value.shape[0], value.shape[1]
    tiles = count * span
    flat = value.reshape(tiles, 8, 128)
    below = jnp.concatenate([x_lo[:, None], value[:, : span - 1]], axis=1)
    above = jnp.concatenate([value[:, 1:], x_hi[:, None]], axis=1)
    row = lax.broadcasted_iota(jnp.int32, (8, 128), 0)
    lane = lanes_of((8, 128))
    before, after, left, right = [], [], [], []
    for i in range(tiles):
        tile = flat[i]
        before.append(
            jnp.where(row == 0, jnp.broadcast_to(y_lo[i], (8, 128)), pltpu.roll(tile, 1, 0))
        )
        after.append(
            jnp.where(row == 7, jnp.broadcast_to(y_hi[i], (8, 128)), pltpu.roll(tile, 7, 0))
        )
        left.append(
            jnp.where(lane == 0, jnp.broadcast_to(z_lo[:, i : i + 1], (8, 128)), pltpu.roll(tile, 1, 1))
        )
        right.append(
            jnp.where(
                lane == 127, jnp.broadcast_to(z_hi[:, i : i + 1], (8, 128)), pltpu.roll(tile, 127, 1)
            )
        )
    join = lambda parts: jnp.stack(parts).reshape(value.shape)
    return above, below, join(after), join(before), join(right), join(left)


def split(value):
    high = value.astype(BF16)
    return high, (value - high.astype(F32)).astype(BF16)


def dot(left, right, dims):
    return lax.dot_general(left, right, (dims, ((), ())), preferred_element_type=F32)


def dot_full(left, right, dims):
    return lax.dot_general(
        left, right, (dims, ((), ())), precision=lax.Precision.HIGHEST, preferred_element_type=F32
    )


NT = ((1,), (1,))
NN = ((1,), (0,))


def kernel(sizes, owners, others, cell_total, noise, basis, cond, react, left_over, chol, proj, *scratch):
    (field, field2, image, stored, react_v, coef, high, low, flat_image, residual,
     x_in1, x_in2, y_out1, y_in1, y_out2, y_in2, z_out1, z_in1, z_out2, z_in2,
     c_data, c_landed, c_crossed, c_result, g_data, g_landed, g_crossed, g_result,
     in_sems, out_sems, h_send1, h_recv1, h_send2, h_recv2, *sum_sems) = scratch
    columns, span = field2.shape[0], field2.shape[1]
    plane = span * 8
    kept = basis.shape[0] // plane
    cells = plane * 128
    tiles = columns * span
    corner = kept - 128
    scale = 1.0 / cell_total

    load_noise = pltpu.make_async_copy(noise, field.at[pl.ds(0, columns)], in_sems.at[0])
    load_cond = pltpu.make_async_copy(cond, field.at[columns], in_sems.at[1])
    load_react = pltpu.make_async_copy(react, react_v, in_sems.at[2])
    load_basis = pltpu.make_async_copy(basis, stored, in_sems.at[3])
    load_noise.start()
    load_cond.start()
    load_react.start()
    load_basis.start()

    barrier = pltpu.get_barrier_semaphore()
    for team in (owners, others):
        def greet(k, team=team):
            pl.semaphore_signal(
                barrier, inc=1, device_id=team.device(team.peer(k)), device_id_type=MESH
            )
        each(team.count, greet)

    rim1 = Rim(field, x_in1, y_out1, y_in1, z_out1, z_in1, h_send1, h_recv1, sizes)
    rim2 = Rim(field2, x_in2, y_out2, y_in2, z_out2, z_in2, h_send2, h_recv2, sizes)
    rim1.blank()
    rim2.blank()
    load_noise.wait()
    load_cond.wait()
    pl.semaphore_wait(barrier, owners.count + others.count - 2)
    rim1.start(0)
    field_flat = field.reshape((columns + 1) * plane, 128)
    y_rows = tiles + span
    y_out1[...] = jnp.zeros(y_out1.shape, F32)
    pack_y(field_flat, y_rows, y_out1)
    rim1.start(1)
    lo, hi = pack_z(field[0:columns].reshape(tiles, 8, 128), tiles)
    z_out1[0, 0], z_out1[1, 0] = lo, hi
    lo, hi = pack_z(field[columns], span)
    z_out1[0, 1], z_out1[1, 1] = lo, hi
    rim1.start(2)

    load_basis.wait()
    spare = high.shape[0] - kept
    high[kept:, :] = jnp.zeros((spare, cells), BF16)
    low[kept:, :] = jnp.zeros((spare, cells), BF16)
    for at in range(plane):
        one, two = split(stored[pl.ds(at, kept, stride=plane), :])
        high[0:kept, at * 128 : (at + 1) * 128] = one
        low[0:kept, at * 128 : (at + 1) * 128] = two

    load_react.wait()
    rim1.arrive()
    theta = field[columns]
    around = neighbours(
        theta[None],
        x_in1[0, columns][None],
        x_in1[1, columns][None],
        [y_in1[0, pl.ds(tiles + i, 1), :] for i in range(span)],
        [y_in1[1, pl.ds(tiles + i, 1), :] for i in range(span)],
        z_in1[0, 1],
        z_in1[1, 1],
    )
    diagonal = react_v[...]
    for face, other in enumerate(around):
        value = 0.5 * (theta + other[0])
        coef[face] = value
        diagonal = diagonal + value
    coef[6] = diagonal

    def apply(source, x_in, y_in, z_in, group):
        start = group * GROUP
        value = source[pl.ds(start, GROUP)]
        shift = (128 - group * (GROUP * span)) % 128
        first = start * span
        around = neighbours(
            value,
            x_in[0, pl.ds(start, GROUP)],
            x_in[1, pl.ds(start, GROUP)],
            [y_in[0, pl.ds(first + i, 1), :] for i in range(GROUP * span)],
            [y_in[1, pl.ds(first + i, 1), :] for i in range(GROUP * span)],
            pltpu.roll(z_in[0, 0], shift, 1) if shift else z_in[0, 0],
            pltpu.roll(z_in[1, 0], shift, 1) if shift else z_in[1, 0],
        )
        result = react_v[...][None] * value
        for face, other in enumerate(around):
            result = result + coef[face][None] * (value - other)
        return start, result

    def first_step(group):
        start, result = apply(field, x_in1, y_in1, z_in1, group)
        field2[pl.ds(start, GROUP)] = result / coef[6][None]

    for group in range(columns // GROUP):
        first_step(group)
    rim2.start(0)
    pack_y(field2.reshape(columns * plane, 128), tiles, y_out2)
    rim2.start(1)
    lo, hi = pack_z(field2[...].reshape(tiles, 8, 128), tiles)
    z_out2[0, 0], z_out2[1, 0] = lo, hi
    rim2.start(2)

    chunk = 1024
    g_one = jnp.zeros((kept, 256), F32)
    g_two = jnp.zeros((kept, 256), F32)
    for at in range(0, cells, chunk):
        right = high[:, at : at + chunk]
        g_one = g_one + dot(high[0:kept, at : at + chunk], right, NT)
        g_two = g_two + dot(low[0:kept, at : at + chunk], right, NT)
    turned = jnp.transpose(jnp.concatenate([g_two, jnp.zeros((256 - kept, 256), F32)], axis=0))
    g_local = g_one + g_two + turned[0:kept]
    for at in range(kept // 8):
        g_data[at] = g_local[8 * at : 8 * at + 8, 0:128]
    for at in range(corner // 8):
        g_data[kept // 8 + at] = g_local[128 + 8 * at : 136 + 8 * at, 128:256]

    c_sum = Sum(owners, others, c_data, c_landed, c_crossed, c_result, sum_sems[0:6])
    g_sum = Sum(owners, others, g_data, g_landed, g_crossed, g_result, sum_sems[6:12])
    g_sum.scatter()

    rim2.arrive()

    def second_step(group):
        start, result = apply(field2, x_in2, y_in2, z_in2, group)
        image[pl.ds(start, GROUP)] = result

    for group in range(columns // GROUP):
        second_step(group)
    g_sum.cross()
    image_rows = image.reshape(columns * plane, 128)
    for at in range(plane):
        value = image_rows[pl.ds(at, columns, stride=plane), :]
        flat_image[:, at * 128 : (at + 1) * 128] = value
        one, two = split(value)
        high[kept : kept + columns, at * 128 : (at + 1) * 128] = one
        low[kept : kept + columns, at * 128 : (at + 1) * 128] = two

    both = jnp.zeros((2 * columns, 256), F32)
    for at in range(0, cells, chunk):
        here = slice(at, at + chunk)
        left = jnp.concatenate([high[kept : kept + columns, here], low[kept : kept + columns, here]], axis=0)
        both = both + dot(left, high[:, here], NT) + dot(left, low[:, here], NT)
    c_local = both[0:columns] + both[columns:]
    for at in range(columns // 8):
        for half in range(2):
            c_data[2 * at + half] = c_local[8 * at : 8 * at + 8, 128 * half : 128 * half + 128]
    c_sum.scatter()
    g_sum.gather()
    c_sum.cross()
    g_sum.finish()
    c_sum.gather()

    def whole(total, rows):
        tiles_of = total[...].reshape(rows // 4, 8, 128)
        return jnp.concatenate(
            [
                jnp.concatenate([tiles_of[2 * at], tiles_of[2 * at + 1]], axis=1)
                for at in range(rows // 8)
            ],
            axis=0,
        )

    g_tiles = g_result[...].reshape(kept // 8 + corner // 8, 8, 128)
    g_left = jnp.concatenate([g_tiles[at] for at in range(kept // 8)], axis=0)
    g_corner = jnp.concatenate([g_tiles[kept // 8 + at] for at in range(corner // 8)], axis=0)
    blank = jnp.zeros((128 - corner, 128), F32)
    g_right = jnp.concatenate(
        [jnp.transpose(jnp.concatenate([g_left[128:], blank], axis=0)), g_corner, blank], axis=0
    )
    g_full = jnp.concatenate([jnp.concatenate([g_left, blank], axis=0), g_right], axis=1)
    square_row = lax.broadcasted_iota(jnp.int32, (256, 256), 0)
    eye = jnp.where((lanes_of((256, 256)) == square_row) & (square_row < kept), 1.0, 0.0)
    h_one = eye.astype(F32) - g_full * scale
    one_high, one_low = split(h_one)

    def times_h(left):
        high_part, low_part = split(left)
        return dot(high_part, one_high, NN) + dot(low_part, one_high, NN) + dot(high_part, one_low, NN)

    h_two = times_h(h_one)
    h_sum = h_one + h_two + times_h(h_two)
    h_high, h_low = split(jnp.concatenate([h_one, h_sum], axis=1))

    c_sum.finish()
    c_full = whole(c_result, columns) * scale
    lane = lanes_of((columns, 256))
    c_one = jnp.where(lane < kept, c_full, 0.0)
    square = c_full[:, kept : kept + columns]
    c_high, c_low = split(c_one)
    c_both = jnp.concatenate([c_high, c_low], axis=0)
    moved = dot(c_both, h_high, NN) + dot(c_both, h_low, NN)
    moved = moved[0:columns] + moved[columns:]
    total = c_one + moved[:, 0:256]
    taken = jnp.concatenate(split(c_one + moved[:, 256:]), axis=0)
    taken = dot(taken, c_high, NT) + dot(taken, c_low, NT)
    gram = square - taken[0:columns] - taken[columns:]
    proj[...] = total[:, 0:kept]

    p_high, p_low = split(total)
    p_both = jnp.concatenate([p_high, p_low], axis=0)[:, 0:kept]
    wide = (columns, 128)
    lane = lanes_of(wide)
    row = lax.broadcasted_iota(jnp.int32, wide, 0)
    table = jnp.where(lane == row + columns, 1.0, 0.0).astype(F32)
    table = table + jnp.concatenate([gram, jnp.zeros((columns, 128 - columns), F32)], axis=1)
    step = 8
    width = cells * step // columns
    writes = []
    for first in range(0, columns, step):
        ahead = [
            jnp.broadcast_to(table[:, first + j : first + j + 1], wide) for j in range(step)
        ]
        for j in range(step):
            k = first + j
            root = lax.rsqrt(ahead[j][k : k + 1, :])
            column = ahead[j] * root
            line = table[k : k + 1, :] * root
            chol[k : k + 1, :] = line
            table = table - column * line
            for m in range(j + 1, step):
                ahead[m] = ahead[m] - column * column[first + m : first + m + 1, :]
        at = first // step * width
        here = slice(at, at + width)
        part = dot(p_both, high[0:kept, here], NN) + dot(p_both, low[0:kept, here], NN)
        residual[:, here] = flat_image[:, here] - part[0:columns] - part[columns:]
        writes.append(
            pltpu.make_async_copy(
                residual.at[:, here], left_over.at[:, here], out_sems.at[first // step]
            )
        )
        writes[-1].start()
    for write in writes:
        write.wait()
    rim1.drain()
    rim2.drain()
    g_sum.drain()
    c_sum.drain()


def finish_kernel(left_over, chol, proj, out, factor, proj_out, rest, table, kept, upper, new, sems):
    columns, span = new.shape[0], new.shape[1]
    width = rest.shape[1] // span
    load_table = pltpu.make_async_copy(chol, table, sems.at[0])
    load_proj = pltpu.make_async_copy(proj, kept, sems.at[1])
    loads = [
        pltpu.make_async_copy(
            left_over.at[:, pl.ds(x * width, width)], rest.at[:, pl.ds(x * width, width)], sems.at[4 + x]
        )
        for x in range(span)
    ]
    load_table.start()
    for load in loads:
        load.start()
    load_proj.start()
    load_table.wait()
    done = table[...]
    row = lax.broadcasted_iota(jnp.int32, done.shape, 0)
    upper[...] = jnp.where(lanes_of(done.shape) >= row, done, 0.0)[:, 0:columns]
    store_factor = pltpu.make_async_copy(upper, factor, sems.at[2])
    store_factor.start()
    load_proj.wait()
    store_proj = pltpu.make_async_copy(kept, proj_out, sems.at[3])
    store_proj.start()
    inverse = jnp.concatenate(split(done[:, columns : 2 * columns]), axis=0)
    rows = new.reshape(columns * span * 8, 128)
    stores = []
    for x in range(span):
        loads[x].wait()
        one, two = split(rest[:, x * width : (x + 1) * width])
        part = dot(inverse, one, NN) + dot(inverse, two, NN)
        part = part[0:columns] + part[columns:]
        for k in range(8):
            rows[pl.ds(x * 8 + k, columns, stride=span * 8), :] = part[:, 128 * k : 128 * k + 128]
        stores.append(pltpu.make_async_copy(new.at[:, x], out.at[:, x], sems.at[4 + span + x]))
        stores[-1].start()
    for store in stores:
        store.wait()
    store_factor.wait()
    store_proj.wait()


def finish(left_over, chol, proj, shape):
    columns, span = shape[0], shape[1]
    return pl.pallas_call(
        finish_kernel,
        out_shape=(
            jax.ShapeDtypeStruct(shape, F32),
            jax.ShapeDtypeStruct((columns, columns), F32),
            jax.ShapeDtypeStruct(proj.shape, F32),
        ),
        in_specs=[pl.BlockSpec(memory_space=pl.ANY)] * 3,
        out_specs=tuple([pl.BlockSpec(memory_space=pl.ANY)] * 3),
        scratch_shapes=[
            pltpu.VMEM(left_over.shape, F32),
            pltpu.VMEM(chol.shape, F32),
            pltpu.VMEM(proj.shape, F32),
            pltpu.VMEM((columns, columns), F32),
            pltpu.VMEM(shape, F32),
            pltpu.SemaphoreType.DMA((4 + 2 * span,)),
        ],
        compiler_params=pltpu.CompilerParams(vmem_limit_bytes=VMEM_GRANT),
        name="new_block",
    )(left_over, chol, proj)


def shards(sizes, noise, basis, cond, react):
    columns, span, rows, lanes = noise.shape
    kept = basis.shape[0]
    plane = span * rows
    cells = plane * lanes
    cell_total = float(cells * sizes["gx"] * sizes["gy"] * sizes["gz"])
    c_tiles, g_tiles = columns // 4, kept // 8 + (kept - 128) // 8
    own, rest, count = [], [], 1
    for axis in ("gx", "gy", "gz"):
        if c_tiles % (count * sizes[axis]) == 0:
            count *= sizes[axis]
            own.append(axis)
        else:
            rest.append(axis)
    owners, others = Team(own, sizes), Team(rest, sizes)
    vmem = lambda *shape: pltpu.VMEM(shape, F32)
    y_rows = -(-(columns + 1) * span // 8) * 8

    def sum_buffers(tiles):
        share = tiles // owners.count
        return [
            vmem(tiles, 8, 128),
            vmem(owners.count, share, 8, 128),
            vmem(others.count, share, 8, 128),
            vmem(owners.count, share, 8, 128),
        ]

    dma = lambda n: pltpu.SemaphoreType.DMA((n,))
    sum_sems = [dma(n) for n in (owners.count, owners.count, others.count, others.count, owners.count, owners.count)]
    scratch = [
        vmem(columns + 1, span, 8, 128),
        vmem(columns, span, 8, 128),
        vmem(columns, span, 8, 128),
        vmem(kept * plane, 128),
        vmem(span, 8, 128),
        vmem(7, span, 8, 128),
        pltpu.VMEM((256, cells), BF16),
        pltpu.VMEM((256, cells), BF16),
        vmem(columns, cells),
        vmem(columns, cells),
        vmem(2, columns + 1, 8, 128),
        vmem(2, columns, 8, 128),
        vmem(2, y_rows, 128),
        vmem(2, y_rows, 128),
        vmem(2, columns * span, 128),
        vmem(2, columns * span, 128),
        vmem(2, 2, 8, 128),
        vmem(2, 2, 8, 128),
        vmem(2, 1, 8, 128),
        vmem(2, 1, 8, 128),
        *sum_buffers(c_tiles),
        *sum_buffers(g_tiles),
        dma(4),
        dma(columns // 8),
        dma(6),
        dma(6),
        dma(6),
        dma(6),
        *sum_sems,
        *sum_sems,
    ]
    left_over, chol, proj = pl.pallas_call(
        functools.partial(kernel, sizes, owners, others, cell_total),
        out_shape=(
            jax.ShapeDtypeStruct((columns, cells), F32),
            jax.ShapeDtypeStruct((columns, 128), F32),
            jax.ShapeDtypeStruct((columns, kept), F32),
        ),
        in_specs=[pl.BlockSpec(memory_space=pl.ANY)] * 4,
        out_specs=(
            pl.BlockSpec(memory_space=pl.ANY),
            pl.BlockSpec(memory_space=pltpu.VMEM),
            pl.BlockSpec(memory_space=pltpu.VMEM),
        ),
        scratch_shapes=scratch,
        compiler_params=pltpu.CompilerParams(
            collective_id=0, has_side_effects=True, vmem_limit_bytes=VMEM_GRANT
        ),
        name="lanczos_step",
    )(noise, basis.reshape(kept * plane, lanes), cond, react)
    out, factor, proj = finish(left_over, chol, proj, noise.shape)
    return out, factor, proj.T


def solution(mesh):
    sizes = dict(mesh.shape)
    return jax.shard_map(
        functools.partial(shards, sizes),
        mesh=mesh,
        in_specs=(
            P(None, "gx", "gy", "gz"),
            P(None, "gx", "gy", "gz"),
            P("gx", "gy", "gz"),
            P("gx", "gy", "gz"),
        ),
        out_specs=(P(None, "gx", "gy", "gz"), P(), P()),
        check_vma=False,
    )
```

```python
import functools

import jax
import jax.numpy as jnp
from jax import lax
from jax.experimental import pallas as pl
from jax.experimental.pallas import tpu as pltpu
from jax.sharding import PartitionSpec as P

MESH = pl.DeviceIdType.MESH
GROUP = 8
VMEM_GRANT = 63 * 1024 * 1024
F32 = jnp.float32
BF16 = jnp.bfloat16


def each(count, body):
    if count <= 8:
        for k in range(1, count):
            body(k)
    else:
        lax.fori_loop(1, count, lambda k, c: (body(k), c)[1], 0)


class Team:
    def __init__(self, axes, sizes):
        self.axes = axes
        self.sizes = sizes
        self.count = 1
        for axis in axes:
            self.count *= sizes[axis]

    def me(self):
        index = 0
        for axis in self.axes:
            index = index * self.sizes[axis] + lax.axis_index(axis)
        return index

    def device(self, index):
        out = {}
        for axis in reversed(self.axes):
            out[axis] = lax.rem(index, self.sizes[axis])
            index = lax.div(index, self.sizes[axis])
        return out

    def peer(self, k):
        return lax.rem(self.me() + k, self.count)


class Sum:
    def __init__(self, owners, others, data, landed, crossed, result, sems):
        self.owners, self.others = owners, others
        self.data, self.landed, self.crossed, self.result = data, landed, crossed, result
        self.sems = sems
        self.share = data.shape[0] // owners.count

    def copy(self, phase, team, src, dst_ref, slot, peer):
        send, recv = self.sems[2 * phase], self.sems[2 * phase + 1]
        return pltpu.make_async_remote_copy(
            src_ref=src,
            dst_ref=dst_ref.at[slot],
            send_sem=send.at[peer],
            recv_sem=recv.at[slot],
            device_id=team.device(peer),
            device_id_type=MESH,
        )

    def piece(self, index):
        return self.data.at[pl.ds(index * self.share, self.share)]

    def scatter(self):
        team, me = self.owners, self.owners.me()

        def go(k):
            peer = team.peer(k)
            self.copy(0, team, self.piece(peer), self.landed, me, peer).start()

        each(team.count, go)
        self.landed[me] = self.data[pl.ds(me * self.share, self.share)]

    def settle(self, phase, team, src, dst_ref):
        def go(k):
            peer = team.peer(k)
            self.copy(phase, team, src, dst_ref, peer, peer).wait_recv()

        each(team.count, go)

    def cross(self):
        self.settle(0, self.owners, self.piece(0), self.landed)
        team, me = self.others, self.others.me()
        total = self.landed[0]
        for k in range(1, self.owners.count):
            total = total + self.landed[k]
        self.crossed[me] = total

        def go(k):
            peer = team.peer(k)
            self.copy(1, team, self.crossed.at[me], self.crossed, me, peer).start()

        each(team.count, go)

    def gather(self):
        self.settle(1, self.others, self.crossed.at[0], self.crossed)
        team, me = self.owners, self.owners.me()
        total = self.crossed[0]
        for k in range(1, self.others.count):
            total = total + self.crossed[k]
        self.result[me] = total

        def go(k):
            peer = team.peer(k)
            self.copy(2, team, self.result.at[me], self.result, me, peer).start()

        each(team.count, go)

    def finish(self):
        self.settle(2, self.owners, self.result.at[0], self.result)

    def drain(self):
        def scattered(k):
            peer = self.owners.peer(k)
            self.copy(0, self.owners, self.piece(0), self.landed, 0, peer).wait_send()

        def crossed(k):
            peer = self.others.peer(k)
            self.copy(1, self.others, self.crossed.at[0], self.crossed, 0, peer).wait_send()

        def gathered(k):
            peer = self.owners.peer(k)
            self.copy(2, self.owners, self.result.at[0], self.result, 0, peer).wait_send()

        each(self.owners.count, scattered)
        each(self.others.count, crossed)
        each(self.owners.count, gathered)


class Rim:
    def __init__(self, field, x_in, y_out, y_in, z_out, z_in, send, recv, sizes):
        self.sizes = sizes
        self.send, self.recv = send, recv
        last = field.shape[1] - 1
        self.routes = (
            ("gx", (field.at[:, 0], field.at[:, last]), x_in),
            ("gy", (y_out.at[0], y_out.at[1]), y_in),
            ("gz", (z_out.at[0], z_out.at[1]), z_in),
        )

    def exists(self, axis, side):
        me = lax.axis_index(axis)
        return me > 0 if side == 0 else me < self.sizes[axis] - 1

    def copy(self, at, side):
        axis, out, into = self.routes[at]
        me = lax.axis_index(axis)
        step = -1 if side == 0 else 1
        return pltpu.make_async_remote_copy(
            src_ref=out[side],
            dst_ref=into.at[1 - side],
            send_sem=self.send.at[2 * at + side],
            recv_sem=self.recv.at[2 * at + 1 - side],
            device_id={axis: me + step},
            device_id_type=MESH,
        )

    def start(self, at):
        axis = self.routes[at][0]
        for side in range(2):
            pl.when(self.exists(axis, side))(lambda at=at, side=side: self.copy(at, side).start())

    def blank(self):
        for axis, _, into in self.routes:
            for side in range(2):
                @pl.when(jnp.logical_not(self.exists(axis, side)))
                def _(into=into, side=side):
                    into[side] = jnp.zeros(into.shape[1:], F32)

    def arrive(self):
        for at in range(3):
            axis = self.routes[at][0]
            for side in range(2):
                pl.when(self.exists(axis, side))(
                    lambda at=at, side=side: self.copy(at, 1 - side).wait_recv()
                )

    def drain(self):
        for at in range(3):
            axis = self.routes[at][0]
            for side in range(2):
                pl.when(self.exists(axis, side))(
                    lambda at=at, side=side: self.copy(at, side).wait_send()
                )


def lanes_of(shape):
    return lax.broadcasted_iota(jnp.int32, shape, len(shape) - 1)


def pack_y(flat, rows, y_out):
    for side, first in ((0, 0), (1, 7)):
        y_out[side, pl.ds(0, rows), :] = flat[pl.ds(first, rows, stride=8), :]


def pack_z(tiles, lanes_total):
    lane = lanes_of((8, 128))
    lo = jnp.zeros((8, 128), F32)
    hi = jnp.zeros((8, 128), F32)
    for i in range(lanes_total):
        tile = tiles[i]
        lo = jnp.where(lane == i, jnp.broadcast_to(tile[:, 0:1], (8, 128)), lo)
        hi = jnp.where(lane == i, jnp.broadcast_to(tile[:, 127:128], (8, 128)), hi)
    return lo, hi


def neighbours(value, x_lo, x_hi, y_lo, y_hi, z_lo, z_hi):
    count, span = value.shape[0], value.shape[1]
    tiles = count * span
    flat = value.reshape(tiles, 8, 128)
    below = jnp.concatenate([x_lo[:, None], value[:, : span - 1]], axis=1)
    above = jnp.concatenate([value[:, 1:], x_hi[:, None]], axis=1)
    row = lax.broadcasted_iota(jnp.int32, (8, 128), 0)
    lane = lanes_of((8, 128))
    before, after, left, right = [], [], [], []
    for i in range(tiles):
        tile = flat[i]
        before.append(
            jnp.where(row == 0, jnp.broadcast_to(y_lo[i], (8, 128)), pltpu.roll(tile, 1, 0))
        )
        after.append(
            jnp.where(row == 7, jnp.broadcast_to(y_hi[i], (8, 128)), pltpu.roll(tile, 7, 0))
        )
        left.append(
            jnp.where(lane == 0, jnp.broadcast_to(z_lo[:, i : i + 1], (8, 128)), pltpu.roll(tile, 1, 1))
        )
        right.append(
            jnp.where(
                lane == 127, jnp.broadcast_to(z_hi[:, i : i + 1], (8, 128)), pltpu.roll(tile, 127, 1)
            )
        )
    join = lambda parts: jnp.stack(parts).reshape(value.shape)
    return above, below, join(after), join(before), join(right), join(left)


def split(value):
    high = value.astype(BF16)
    return high, (value - high.astype(F32)).astype(BF16)


def dot(left, right, dims):
    return lax.dot_general(left, right, (dims, ((), ())), preferred_element_type=F32)


def dot_full(left, right, dims):
    return lax.dot_general(
        left, right, (dims, ((), ())), precision=lax.Precision.HIGHEST, preferred_element_type=F32
    )


NT = ((1,), (1,))
NN = ((1,), (0,))


def kernel(sizes, owners, others, cell_total, noise, basis, cond, react, left_over, chol, proj, *scratch):
    (field, field2, image, stored, react_v, coef, high, low, flat_image, residual,
     x_in1, x_in2, y_out1, y_in1, y_out2, y_in2, z_out1, z_in1, z_out2, z_in2,
     c_data, c_landed, c_crossed, c_result, g_data, g_landed, g_crossed, g_result,
     in_sems, out_sems, h_send1, h_recv1, h_send2, h_recv2, *sum_sems) = scratch
    columns, span = field2.shape[0], field2.shape[1]
    plane = span * 8
    kept = basis.shape[0] // plane
    cells = plane * 128
    tiles = columns * span
    corner = kept - 128
    scale = 1.0 / cell_total

    load_noise = pltpu.make_async_copy(noise, field.at[pl.ds(0, columns)], in_sems.at[0])
    load_cond = pltpu.make_async_copy(cond, field.at[columns], in_sems.at[1])
    load_react = pltpu.make_async_copy(react, react_v, in_sems.at[2])
    load_basis = pltpu.make_async_copy(basis, stored, in_sems.at[3])
    load_noise.start()
    load_cond.start()
    load_react.start()
    load_basis.start()

    barrier = pltpu.get_barrier_semaphore()
    for team in (owners, others):
        def greet(k, team=team):
            pl.semaphore_signal(
                barrier, inc=1, device_id=team.device(team.peer(k)), device_id_type=MESH
            )
        each(team.count, greet)

    rim1 = Rim(field, x_in1, y_out1, y_in1, z_out1, z_in1, h_send1, h_recv1, sizes)
    rim2 = Rim(field2, x_in2, y_out2, y_in2, z_out2, z_in2, h_send2, h_recv2, sizes)
    rim1.blank()
    rim2.blank()
    load_noise.wait()
    load_cond.wait()
    pl.semaphore_wait(barrier, owners.count + others.count - 2)
    rim1.start(0)
    field_flat = field.reshape((columns + 1) * plane, 128)
    y_rows = tiles + span
    y_out1[...] = jnp.zeros(y_out1.shape, F32)
    pack_y(field_flat, y_rows, y_out1)
    rim1.start(1)
    lo, hi = pack_z(field[0:columns].reshape(tiles, 8, 128), tiles)
    z_out1[0, 0], z_out1[1, 0] = lo, hi
    lo, hi = pack_z(field[columns], span)
    z_out1[0, 1], z_out1[1, 1] = lo, hi
    rim1.start(2)

    load_basis.wait()
    spare = high.shape[0] - kept
    high[kept:, :] = jnp.zeros((spare, cells), BF16)
    low[kept:, :] = jnp.zeros((spare, cells), BF16)
    for at in range(plane):
        one, two = split(stored[pl.ds(at, kept, stride=plane), :])
        high[0:kept, at * 128 : (at + 1) * 128] = one
        low[0:kept, at * 128 : (at + 1) * 128] = two

    load_react.wait()
    rim1.arrive()
    theta = field[columns]
    around = neighbours(
        theta[None],
        x_in1[0, columns][None],
        x_in1[1, columns][None],
        [y_in1[0, pl.ds(tiles + i, 1), :] for i in range(span)],
        [y_in1[1, pl.ds(tiles + i, 1), :] for i in range(span)],
        z_in1[0, 1],
        z_in1[1, 1],
    )
    diagonal = react_v[...]
    for face, other in enumerate(around):
        value = 0.5 * (theta + other[0])
        coef[face] = value
        diagonal = diagonal + value
    coef[6] = diagonal

    def apply(source, x_in, y_in, z_in, group):
        start = group * GROUP
        value = source[pl.ds(start, GROUP)]
        shift = (128 - group * (GROUP * span)) % 128
        first = start * span
        around = neighbours(
            value,
            x_in[0, pl.ds(start, GROUP)],
            x_in[1, pl.ds(start, GROUP)],
            [y_in[0, pl.ds(first + i, 1), :] for i in range(GROUP * span)],
            [y_in[1, pl.ds(first + i, 1), :] for i in range(GROUP * span)],
            pltpu.roll(z_in[0, 0], shift, 1) if shift else z_in[0, 0],
            pltpu.roll(z_in[1, 0], shift, 1) if shift else z_in[1, 0],
        )
        result = react_v[...][None] * value
        for face, other in enumerate(around):
            result = result + coef[face][None] * (value - other)
        return start, result

    def first_step(group):
        start, result = apply(field, x_in1, y_in1, z_in1, group)
        field2[pl.ds(start, GROUP)] = result / coef[6][None]

    for group in range(columns // GROUP):
        first_step(group)
    rim2.start(0)
    pack_y(field2.reshape(columns * plane, 128), tiles, y_out2)
    rim2.start(1)
    lo, hi = pack_z(field2[...].reshape(tiles, 8, 128), tiles)
    z_out2[0, 0], z_out2[1, 0] = lo, hi
    rim2.start(2)

    chunk = 1024
    g_both = jnp.zeros((2 * kept, 256), F32)
    for at in range(0, cells, chunk):
        here = slice(at, at + chunk)
        left = jnp.concatenate([high[0:kept, here], low[0:kept, here]], axis=0)
        g_both = g_both + dot(left, high[:, here], NT)
    g_one, g_two = g_both[0:kept], g_both[kept:]
    turned = jnp.transpose(jnp.concatenate([g_two, jnp.zeros((256 - kept, 256), F32)], axis=0))
    g_local = g_one + g_two + turned[0:kept]
    for at in range(kept // 8):
        g_data[at] = g_local[8 * at : 8 * at + 8, 0:128]
    for at in range(corner // 8):
        g_data[kept // 8 + at] = g_local[128 + 8 * at : 136 + 8 * at, 128:256]

    c_sum = Sum(owners, others, c_data, c_landed, c_crossed, c_result, sum_sems[0:6])
    g_sum = Sum(owners, others, g_data, g_landed, g_crossed, g_result, sum_sems[6:12])
    g_sum.scatter()

    rim2.arrive()

    def second_step(group):
        start, result = apply(field2, x_in2, y_in2, z_in2, group)
        image[pl.ds(start, GROUP)] = result

    for group in range(columns // GROUP):
        second_step(group)
    g_sum.cross()
    image_rows = image.reshape(columns * plane, 128)
    for at in range(plane):
        value = image_rows[pl.ds(at, columns, stride=plane), :]
        flat_image[:, at * 128 : (at + 1) * 128] = value
        one, two = split(value)
        high[kept : kept + columns, at * 128 : (at + 1) * 128] = one
        low[kept : kept + columns, at * 128 : (at + 1) * 128] = two

    both = jnp.zeros((512, 128), F32)
    unused = jnp.zeros((128 - 2 * columns, chunk), BF16)
    for at in range(0, cells, chunk):
        here = slice(at, at + chunk)
        right = [high[kept : kept + columns, here], low[kept : kept + columns, here], unused]
        left = jnp.concatenate([high[:, here], low[:, here]], axis=0)
        both = both + dot(left, jnp.concatenate(right, axis=0), NT)
    both = jnp.transpose(both[0:256] + both[256:])
    c_local = both[0:columns] + both[columns : 2 * columns]
    for at in range(columns // 8):
        for half in range(2):
            c_data[2 * at + half] = c_local[8 * at : 8 * at + 8, 128 * half : 128 * half + 128]
    c_sum.scatter()
    g_sum.gather()
    c_sum.cross()
    g_sum.finish()
    c_sum.gather()

    def whole(total, rows):
        tiles_of = total[...].reshape(rows // 4, 8, 128)
        return jnp.concatenate(
            [
                jnp.concatenate([tiles_of[2 * at], tiles_of[2 * at + 1]], axis=1)
                for at in range(rows // 8)
            ],
            axis=0,
        )

    g_tiles = g_result[...].reshape(kept // 8 + corner // 8, 8, 128)
    g_left = jnp.concatenate([g_tiles[at] for at in range(kept // 8)], axis=0)
    g_corner = jnp.concatenate([g_tiles[kept // 8 + at] for at in range(corner // 8)], axis=0)
    blank = jnp.zeros((128 - corner, 128), F32)
    g_right = jnp.concatenate(
        [jnp.transpose(jnp.concatenate([g_left[128:], blank], axis=0)), g_corner, blank], axis=0
    )
    g_full = jnp.concatenate([jnp.concatenate([g_left, blank], axis=0), g_right], axis=1)
    square_row = lax.broadcasted_iota(jnp.int32, (256, 256), 0)
    eye = jnp.where((lanes_of((256, 256)) == square_row) & (square_row < kept), 1.0, 0.0)
    h_one = eye.astype(F32) - g_full * scale
    one_high, one_low = split(h_one)

    def times_h(left):
        high_part, low_part = split(left)
        return dot(high_part, one_high, NN) + dot(low_part, one_high, NN) + dot(high_part, one_low, NN)

    h_two = times_h(h_one)
    h_sum = h_one + h_two + times_h(h_two)
    h_high, h_low = split(jnp.concatenate([h_one, h_sum], axis=1))

    c_sum.finish()
    c_full = whole(c_result, columns) * scale
    lane = lanes_of((columns, 256))
    c_one = jnp.where(lane < kept, c_full, 0.0)
    square = c_full[:, kept : kept + columns]
    c_high, c_low = split(c_one)
    c_both = jnp.concatenate([c_high, c_low], axis=0)
    moved = dot(c_both, h_high, NN) + dot(c_both, h_low, NN)
    moved = moved[0:columns] + moved[columns:]
    total = c_one + moved[:, 0:256]
    taken = jnp.concatenate(split(c_one + moved[:, 256:]), axis=0)
    taken = dot(taken, c_high, NT) + dot(taken, c_low, NT)
    gram = square - taken[0:columns] - taken[columns:]
    proj[...] = total[:, 0:kept]

    p_high, p_low = split(total)
    p_both = jnp.concatenate([p_high, p_low], axis=0)[:, 0:kept]
    wide = (columns, 128)
    lane = lanes_of(wide)
    row = lax.broadcasted_iota(jnp.int32, wide, 0)
    table = jnp.where(lane == row + columns, 1.0, 0.0).astype(F32)
    table = table + jnp.concatenate([gram, jnp.zeros((columns, 128 - columns), F32)], axis=1)
    step = 8
    width = cells * step // columns
    writes = []
    for first in range(0, columns, step):
        ahead = [
            jnp.broadcast_to(table[:, first + j : first + j + 1], wide) for j in range(step)
        ]
        for j in range(step):
            k = first + j
            root = lax.rsqrt(ahead[j][k : k + 1, :])
            column = ahead[j] * root
            line = table[k : k + 1, :] * root
            chol[k : k + 1, :] = line
            table = table - column * line
            for m in range(j + 1, step):
                ahead[m] = ahead[m] - column * column[first + m : first + m + 1, :]
        at = first // step * width
        here = slice(at, at + width)
        part = dot(p_both, high[0:kept, here], NN) + dot(p_both, low[0:kept, here], NN)
        residual[:, here] = flat_image[:, here] - part[0:columns] - part[columns:]
        writes.append(
            pltpu.make_async_copy(
                residual.at[:, here], left_over.at[:, here], out_sems.at[first // step]
            )
        )
        writes[-1].start()
    for write in writes:
        write.wait()
    rim1.drain()
    rim2.drain()
    g_sum.drain()
    c_sum.drain()


def finish_kernel(left_over, chol, proj, out, factor, proj_out, rest, table, kept, upper, new, sems):
    columns, span = new.shape[0], new.shape[1]
    width = rest.shape[1] // span
    load_table = pltpu.make_async_copy(chol, table, sems.at[0])
    load_proj = pltpu.make_async_copy(proj, kept, sems.at[1])
    loads = [
        pltpu.make_async_copy(
            left_over.at[:, pl.ds(x * width, width)], rest.at[:, pl.ds(x * width, width)], sems.at[4 + x]
        )
        for x in range(span)
    ]
    load_table.start()
    for load in loads:
        load.start()
    load_proj.start()
    load_table.wait()
    done = table[...]
    row = lax.broadcasted_iota(jnp.int32, done.shape, 0)
    upper[...] = jnp.where(lanes_of(done.shape) >= row, done, 0.0)[:, 0:columns]
    store_factor = pltpu.make_async_copy(upper, factor, sems.at[2])
    store_factor.start()
    load_proj.wait()
    store_proj = pltpu.make_async_copy(kept, proj_out, sems.at[3])
    store_proj.start()
    inverse = jnp.concatenate(split(done[:, columns : 2 * columns]), axis=0)
    rows = new.reshape(columns * span * 8, 128)
    stores = []
    for x in range(span):
        loads[x].wait()
        one, two = split(rest[:, x * width : (x + 1) * width])
        part = dot(inverse, one, NN) + dot(inverse, two, NN)
        part = part[0:columns] + part[columns:]
        for k in range(8):
            rows[pl.ds(x * 8 + k, columns, stride=span * 8), :] = part[:, 128 * k : 128 * k + 128]
        stores.append(pltpu.make_async_copy(new.at[:, x], out.at[:, x], sems.at[4 + span + x]))
        stores[-1].start()
    for store in stores:
        store.wait()
    store_factor.wait()
    store_proj.wait()


def finish(left_over, chol, proj, shape):
    columns, span = shape[0], shape[1]
    return pl.pallas_call(
        finish_kernel,
        out_shape=(
            jax.ShapeDtypeStruct(shape, F32),
            jax.ShapeDtypeStruct((columns, columns), F32),
            jax.ShapeDtypeStruct(proj.shape, F32),
        ),
        in_specs=[pl.BlockSpec(memory_space=pl.ANY)] * 3,
        out_specs=tuple([pl.BlockSpec(memory_space=pl.ANY)] * 3),
        scratch_shapes=[
            pltpu.VMEM(left_over.shape, F32),
            pltpu.VMEM(chol.shape, F32),
            pltpu.VMEM(proj.shape, F32),
            pltpu.VMEM((columns, columns), F32),
            pltpu.VMEM(shape, F32),
            pltpu.SemaphoreType.DMA((4 + 2 * span,)),
        ],
        compiler_params=pltpu.CompilerParams(vmem_limit_bytes=VMEM_GRANT),
        name="new_block",
    )(left_over, chol, proj)


def shards(sizes, noise, basis, cond, react):
    columns, span, rows, lanes = noise.shape
    kept = basis.shape[0]
    plane = span * rows
    cells = plane * lanes
    cell_total = float(cells * sizes["gx"] * sizes["gy"] * sizes["gz"])
    c_tiles, g_tiles = columns // 4, kept // 8 + (kept - 128) // 8
    own, rest, count = [], [], 1
    for axis in ("gx", "gy", "gz"):
        if c_tiles % (count * sizes[axis]) == 0:
            count *= sizes[axis]
            own.append(axis)
        else:
            rest.append(axis)
    owners, others = Team(own, sizes), Team(rest, sizes)
    vmem = lambda *shape: pltpu.VMEM(shape, F32)
    y_rows = -(-(columns + 1) * span // 8) * 8

    def sum_buffers(tiles):
        share = tiles // owners.count
        return [
            vmem(tiles, 8, 128),
            vmem(owners.count, share, 8, 128),
            vmem(others.count, share, 8, 128),
            vmem(owners.count, share, 8, 128),
        ]

    dma = lambda n: pltpu.SemaphoreType.DMA((n,))
    sum_sems = [dma(n) for n in (owners.count, owners.count, others.count, others.count, owners.count, owners.count)]
    scratch = [
        vmem(columns + 1, span, 8, 128),
        vmem(columns, span, 8, 128),
        vmem(columns, span, 8, 128),
        vmem(kept * plane, 128),
        vmem(span, 8, 128),
        vmem(7, span, 8, 128),
        pltpu.VMEM((256, cells), BF16),
        pltpu.VMEM((256, cells), BF16),
        vmem(columns, cells),
        vmem(columns, cells),
        vmem(2, columns + 1, 8, 128),
        vmem(2, columns, 8, 128),
        vmem(2, y_rows, 128),
        vmem(2, y_rows, 128),
        vmem(2, columns * span, 128),
        vmem(2, columns * span, 128),
        vmem(2, 2, 8, 128),
        vmem(2, 2, 8, 128),
        vmem(2, 1, 8, 128),
        vmem(2, 1, 8, 128),
        *sum_buffers(c_tiles),
        *sum_buffers(g_tiles),
        dma(4),
        dma(columns // 8),
        dma(6),
        dma(6),
        dma(6),
        dma(6),
        *sum_sems,
        *sum_sems,
    ]
    left_over, chol, proj = pl.pallas_call(
        functools.partial(kernel, sizes, owners, others, cell_total),
        out_shape=(
            jax.ShapeDtypeStruct((columns, cells), F32),
            jax.ShapeDtypeStruct((columns, 128), F32),
            jax.ShapeDtypeStruct((columns, kept), F32),
        ),
        in_specs=[pl.BlockSpec(memory_space=pl.ANY)] * 4,
        out_specs=(
            pl.BlockSpec(memory_space=pl.ANY),
            pl.BlockSpec(memory_space=pltpu.VMEM),
            pl.BlockSpec(memory_space=pltpu.VMEM),
        ),
        scratch_shapes=scratch,
        compiler_params=pltpu.CompilerParams(
            collective_id=0, has_side_effects=True, vmem_limit_bytes=VMEM_GRANT
        ),
        name="lanczos_step",
    )(noise, basis.reshape(kept * plane, lanes), cond, react)
    out, factor, proj = finish(left_over, chol, proj, noise.shape)
    return out, factor, proj.T


def solution(mesh):
    sizes = dict(mesh.shape)
    return jax.shard_map(
        functools.partial(shards, sizes),
        mesh=mesh,
        in_specs=(
            P(None, "gx", "gy", "gz"),
            P(None, "gx", "gy", "gz"),
            P("gx", "gy", "gz"),
            P("gx", "gy", "gz"),
        ),
        out_specs=(P(None, "gx", "gy", "gz"), P(), P()),
        check_vma=False,
    )
```
